32 devices in a mesh: label: 16 (over z, x, core), doc: 2 (over y).
Axes of the slice: x: 2, y: 2, z: 4, core: 2. Of those that a mesh axis runs over, the one named last changes fastest.
Arguments:
- tokens: bfloat16 [32, 128, 768], P(('label', 'doc')), may hold values from -6 to 6
- norm_gains: float32 [2, 768], replicated, may hold values from 0.1 to 1.9
- enc_weight: bfloat16 [768, 768], replicated, may hold values from -0.21875 to 0.21875
- head_weight: bfloat16 [16384, 768], P(('label', 'doc')), may hold values from -0.59765625 to 0.59765625
- head_bias: bfloat16 [16384], P(('label', 'doc')), may hold values from -12 to -7
- positives: int32 [32, 8], P(('label', 'doc')), may hold values from -1 to 16383, as said below
Outputs:
- row_grad: float32 [32, 768], P(('label', 'doc'))
- weight_grad: float32 [768, 768], replicated
- gain_grads: float32 [2, 768], replicated
The draws below stay inside these ranges and needn't reach their ends.
Inputs may be any that keep to these rules, and one draw needn't show every extreme that they name: `positives`: each document lists 3 to 8 label ids at the front of its row and -1 in the remaining slots; an id may repeat within a row and then counts once.
All inputs are finite; a program needn't handle non-finite values.
Results may differ from the reference program's by a relative error of at most 0.0025.
The reference program's roundings to bfloat16 on the way (of `act_in`, `embed_bf` and `d_logit`) count: a program that leaves them out, or rounds other values in their place, can miss the bound.
Values may be sent and summed in bfloat16 or wider, within the bound.
No kernel may reach another device: no remote copies, remote signals or barrier semaphores. Data moves between devices by JAX's collectives and lax.ppermute only.
A program may use at most 64 MiB of HBM per device.

```python
import jax
import jax.numpy as jnp
from jax import lax

D = 768
SEQ = 128
DOC_DEV = 1
L_STORE = 512
POS = 8
DOCS = 32
LABELS = 16384
N_LABEL = 16
N_DOC = 2


def draw_positives(key, part):
    count_key, label_key = jax.random.split(jax.random.fold_in(key, 17))
    counts = jax.random.randint(count_key, (DOCS, 1), 3, POS + 1)
    label_ids = jax.random.randint(label_key, (DOCS, POS), 0, LABELS)
    slots = jnp.arange(POS)[None, :]
    return jnp.where(slots < counts, label_ids, -1).astype(jnp.int32)


def shard_levels(rng, dims, cuts, smallest, largest):
    def one(axis_at, parts):
        draws = jax.random.uniform(jax.random.fold_in(jax.random.fold_in(rng, 6), axis_at), (parts,), jnp.float32, smallest / len(cuts), largest / len(cuts))
        return jnp.repeat(jnp.exp(draws), dims[axis_at] // parts).reshape((-1,) + (1,) * (len(dims) - axis_at - 1))

    level = one(*cuts[0])
    for cut in cuts[1:]:
        level = level * one(*cut)
    return level


def gaussian(key, dims, scale, bound, pieces=(), kind=jnp.bfloat16):
    array = scale * jax.random.normal(key, dims, jnp.float32)
    if pieces:
        array = array * shard_levels(key, dims, pieces, -0.22, 0.18)
    return jnp.clip(array, -bound, bound).astype(kind)


def setup_inputs(seed: int = 0) -> dict:
    seeds = jax.random.split(jax.random.key(seed), 7)
    return {
        "tokens": gaussian(seeds[0], (DOCS, SEQ, D), 1.0, 6.0, ((0, 32),)),
        "norm_gains": jnp.clip(1.0 + 0.18 * jax.random.normal(seeds[1], (2, D), jnp.float32), 0.1, 1.9),
        "enc_weight": gaussian(seeds[2], (D, D), D ** -0.5, 0.21875),
        "head_weight": gaussian(seeds[3], (LABELS, D), 0.1, 0.59765625, ((0, 32),)),
        "head_bias": jnp.clip(-12.0 + 5.0 * jax.random.uniform(seeds[4], (LABELS,), jnp.float32) ** shard_levels(seeds[4], (LABELS,), ((0, 32),), -0.2, 0.2), -12.0, -7.0).astype(jnp.bfloat16),
        "positives": draw_positives(jax.random.fold_in(seeds[6], 71), 0),
    }


epsilon = 1e-05

def normalize(values):
    center = values - lax.optimization_barrier(jnp.mean(values, axis=-1, keepdims=True))
    inverse = lax.rsqrt(lax.optimization_barrier(jnp.mean(center * center, axis=-1, keepdims=True)) + epsilon)
    return (center * inverse, inverse)

def encode(tok_block, gains, enc_weight):
    width = tok_block.shape[-1]
    tok_flat = tok_block.reshape(-1, width).astype(jnp.float32)
    normed_in, _ = normalize(tok_flat)
    act_in = (normed_in * gains[0]).astype(jnp.bfloat16)
    pre_act = jnp.dot(act_in, enc_weight, preferred_element_type=jnp.float32)
    hidden = tok_flat + jax.nn.gelu(pre_act)
    pooled = lax.optimization_barrier(jnp.mean(hidden.reshape(tok_block.shape[0], tok_block.shape[1], width), axis=1))
    normed_out, inv_out = normalize(pooled)
    return (normed_out * gains[1], (normed_in, act_in, pre_act, normed_out, inv_out))

def encode_back(cotangent, saved, gains, enc_weight, seq_len):
    normed_in, act_in, pre_act, normed_out, inv_out = saved
    gain_out_grad = lax.optimization_barrier(jnp.sum(cotangent * normed_out, axis=0))
    d_normed = cotangent * gains[1]
    d_pooled = inv_out * (d_normed - lax.optimization_barrier(jnp.mean(d_normed, axis=-1, keepdims=True)) - normed_out * lax.optimization_barrier(jnp.mean(d_normed * normed_out, axis=-1, keepdims=True)))
    spread_grad = jnp.broadcast_to((d_pooled / seq_len)[:, None, :], (d_pooled.shape[0], seq_len, d_pooled.shape[1])).reshape(pre_act.shape)
    _, gelu_back = jax.vjp(jax.nn.gelu, pre_act)
    d_pre = gelu_back(spread_grad)[0]
    weight_grad = lax.dot_general(act_in.astype(jnp.float32), d_pre, (((0,), (0,)), ((), ())), precision=lax.Precision.HIGHEST, preferred_element_type=jnp.float32)
    d_act = lax.dot_general(d_pre, enc_weight.astype(jnp.float32), (((1,), (1,)), ((), ())), precision=lax.Precision.HIGHEST, preferred_element_type=jnp.float32)
    gain_in_grad = lax.optimization_barrier(jnp.sum(d_act * normed_in, axis=0))
    return (weight_grad, jnp.stack([gain_in_grad, gain_out_grad]))

def head_block(embed_bf, label_lists, weight_block, bias_block, first_label):
    logits = lax.dot_general(embed_bf, weight_block, (((1,), (1,)), ((), ())), preferred_element_type=jnp.float32)
    logits = logits + bias_block.astype(jnp.float32)[None, :]
    label_ids = first_label + jnp.arange(weight_block.shape[0], dtype=jnp.int32)
    target = jnp.any(label_lists[:, :, None] == label_ids[None, None, :], axis=1).astype(jnp.float32)
    d_logit = (jax.nn.sigmoid(logits) - target).astype(jnp.bfloat16)
    return jnp.dot(d_logit, weight_block, preferred_element_type=jnp.float32)

def reference(tokens, norm_gains, enc_weight, head_weight, head_bias, positives):
    tok_blocks = tokens.reshape(N_LABEL * N_DOC, DOC_DEV, SEQ, D)
    embed = lax.map(lambda tok_block: encode(tok_block, norm_gains, enc_weight)[0], tok_blocks).reshape(DOCS, D)
    embed_bf = embed.astype(jnp.bfloat16)
    span = L_STORE * N_DOC
    weight_blocks = head_weight.reshape(N_LABEL, span, D)
    bias_blocks = head_bias.reshape(N_LABEL, span)

    def add_block(total, inputs):
        block_index, weight_block, bias_block = inputs
        first_label = (block_index * span).astype(jnp.int32)
        return (total + head_block(embed_bf, positives, weight_block, bias_block, first_label), None)
    row_grad, _ = lax.scan(add_block, jnp.zeros((DOCS, D), jnp.float32), (jnp.arange(N_LABEL, dtype=jnp.int32), weight_blocks, bias_blocks))
    cotangent = row_grad

    def back_block(carry, inputs):
        tok_block, cot_block = inputs
        _, saved = encode(tok_block, norm_gains, enc_weight)
        weight_part, gain_part = encode_back(cot_block, saved, norm_gains, enc_weight, SEQ)
        return ((carry[0] + weight_part, carry[1] + gain_part), None)
    (weight_grad, gain_grads), _ = lax.scan(back_block, (jnp.zeros((D, D), jnp.float32), jnp.zeros((2, D), jnp.float32)), (tok_blocks, cotangent.reshape(N_LABEL * N_DOC, DOC_DEV, D)))
    return (row_grad, weight_grad, gain_grads)
```

```python
import functools
import math

import jax
import jax.numpy as jnp
from jax import lax
from jax.experimental import pallas as pl
from jax.experimental.pallas import tpu as pltpu
from jax.sharding import PartitionSpec as P

epsilon = 1e-05
AXES = ("label", "doc")
PIECE_BITS = 8
PIECE = 1 << PIECE_BITS
DIGITS = 3
GATHER_LIMIT = 8 << 20
f32, bf16 = jnp.float32, jnp.bfloat16


def encode_rows(tok, gains, weight):
    mean = jnp.mean(tok, axis=-1, keepdims=True)
    center = tok - mean
    inverse = lax.rsqrt(jnp.mean(center * center, axis=-1, keepdims=True) + epsilon)
    act = (center * inverse * gains[0:1]).astype(bf16)
    pre = jnp.dot(act, weight, preferred_element_type=f32)
    scale = math.sqrt(2.0 / math.pi)
    square = pre * pre
    bend = jnp.tanh(pre * (scale + (scale * 0.044715) * square))
    half = 0.5 * pre
    gelu = half + half * bend
    tilt = 0.5 * bend + half * (1.0 - bend * bend) * (scale + (3.0 * scale * 0.044715) * square)
    return act, tilt, jnp.sum(tok + gelu, axis=0, keepdims=True), jnp.sum(act.astype(f32), axis=0, keepdims=True)


def norm_row(pooled):
    center = pooled - jnp.mean(pooled, axis=-1, keepdims=True)
    inverse = lax.rsqrt(jnp.mean(center * center, axis=-1, keepdims=True) + epsilon)
    return center * inverse, inverse


def place(device, core):
    return (device // (2 * core)) * core + device % core


def number():
    return lax.axis_index("label") * lax.axis_size("doc") + lax.axis_index("doc")


def encode_into(layout, toks, gains, weight, act_ref, tilt_ref, row_ref):
    at = 0
    for d, doc in enumerate(layout):
        seq = sum(rows for _, _, rows in doc)
        total, acts = 0.0, 0.0
        for operand, first, rows in doc:
            for start in range(0, rows, seq // 2):
                span = min(seq // 2, rows)
                tok = toks[operand][first + start : first + start + span, :].astype(f32)
                act, tilt, part, sums = encode_rows(tok, gains, weight)
                act_ref[at : at + span, :] = act
                tilt_ref[at : at + span, :] = tilt
                total, acts, at = total + part, acts + sums, at + span
        normed, inverse = norm_row(total * (1.0 / seq))
        row_ref[d, 0:1, :] = normed
        row_ref[d, 1:2, :] = jnp.broadcast_to(inverse, normed.shape)
        row_ref[d, 2:3, :] = acts
    return normed


def first_kernel(*refs):
    sources, (act_ref, tilt_ref, row_ref, embed_ref), held, (digits, sems) = refs[:4], refs[4:8], refs[8:12], refs[12:]
    copies = [pltpu.make_async_copy(a, b, sems.at[k]) for k, (a, b) in enumerate(zip(sources, held, strict=True))]
    for copy in copies:
        copy.start()
    for copy in copies:
        copy.wait()
    tok, gains_ref, weight_ref, listed_ref = held
    gains = gains_ref[...]
    seq, width = tok.shape
    slots = listed_ref.shape[1]
    normed = encode_into([[(0, 0, seq)]], [tok], gains, weight_ref[...], act_ref, tilt_ref, row_ref)
    embed = normed * gains[1:2]
    digits[...] = jnp.zeros_like(digits)
    shifted = listed_ref[...] + 1
    for k in range(DIGITS):
        digit = jnp.bitwise_and(jnp.right_shift(shifted, PIECE_BITS * (DIGITS - 1 - k)), PIECE - 1)
        digits[:, k * slots : (k + 1) * slots] = digit.astype(f32)
    lanes = [embed[:, k * 128 : (k + 1) * 128] for k in range(width // 128)] + [digits[...]]
    lanes += [jnp.zeros((1, 128), f32)] * (embed_ref.shape[1] - len(lanes))
    block = jnp.concatenate(lanes, axis=0).astype(bf16)
    embed_ref[...] = jnp.broadcast_to(block[None], embed_ref.shape)


def encode_kernel(layout, *refs):
    toks, (gains_ref, weight_ref, act_ref, tilt_ref, row_ref) = refs[:-5], refs[-5:]
    encode_into(layout, toks, gains_ref[...], weight_ref[...], act_ref, tilt_ref, row_ref)


def encode_shapes(rows, docs, width):
    return [
        jax.ShapeDtypeStruct((rows, width), bf16),
        jax.ShapeDtypeStruct((rows, width), f32),
        jax.ShapeDtypeStruct((docs, 8, width), f32),
    ]


def first_call(own, gains, weight, listed, copies):
    seq, width = own.shape
    sources = [own, gains, weight, listed]
    deep = -(-(width // 128 + 1) // 8) * 8
    return pl.pallas_call(
        first_kernel,
        out_shape=encode_shapes(seq, 1, width) + [jax.ShapeDtypeStruct((copies, deep, 128), bf16)],
        in_specs=[pl.BlockSpec(memory_space=pl.ANY)] * 4,
        scratch_shapes=[pltpu.VMEM(a.shape, a.dtype) for a in sources]
        + [pltpu.VMEM((1, 128), f32), pltpu.SemaphoreType.DMA((4,))],
        compiler_params=pltpu.CompilerParams(vmem_limit_bytes=10 << 20),
        name="first",
    )(*sources)


def encode_call(arrays, layout, gains, weight):
    rows = sum(piece[2] for doc in layout for piece in doc)
    return pl.pallas_call(
        functools.partial(encode_kernel, layout),
        out_shape=encode_shapes(rows, len(layout), gains.shape[1]),
        compiler_params=pltpu.CompilerParams(vmem_limit_bytes=14 << 20),
        name="encode",
    )(*arrays, gains, weight)


def join_kernel(pieces, *refs):
    out_ref = refs[-1]
    at = 0
    for operand, first, rows in pieces:
        out_ref[at : at + rows, :] = refs[operand][first : first + rows, :]
        at += rows


def join(parts, tied=()):
    arrays, pieces = [], []
    for array, first, rows in parts:
        known = [k for k, a in enumerate(arrays) if a is array]
        if not known:
            known = [len(arrays)]
            arrays.append(array)
        pieces.append((known[0], first, rows))
    vmem, anywhere = pl.BlockSpec(memory_space=pltpu.VMEM), pl.BlockSpec(memory_space=pl.ANY)
    return pl.pallas_call(
        functools.partial(join_kernel, pieces),
        out_shape=jax.ShapeDtypeStruct((sum(p[2] for p in pieces), arrays[0].shape[1]), arrays[0].dtype),
        in_specs=[vmem] * len(arrays) + [anywhere] * len(tied),
        compiler_params=pltpu.CompilerParams(vmem_limit_bytes=4 << 20),
        name="join",
    )(*arrays, *tied)


def add_kernel(count, *refs):
    parts = [ref[...] for ref in refs[:count]]
    while len(parts) > 1:
        parts = [parts[i] + parts[i + 1] for i in range(0, len(parts), 2)]
    refs[-1][...] = parts[0]


def add(parts, tied=()):
    vmem, anywhere = pl.BlockSpec(memory_space=pltpu.VMEM), pl.BlockSpec(memory_space=pl.ANY)
    return pl.pallas_call(
        functools.partial(add_kernel, len(parts)),
        out_shape=jax.ShapeDtypeStruct(parts[0].shape, parts[0].dtype),
        in_specs=[vmem] * len(parts) + [anywhere] * len(tied),
        compiler_params=pltpu.CompilerParams(vmem_limit_bytes=4 << 20),
        name="add",
    )(*parts, *tied)


def head_kernel(slots, rows_ref, weight_ref, bias_ref, mine_ref, other_ref, rows, part):
    labels, width = weight_ref.shape
    lanes = width // 128 + 1
    me, core = number(), lax.axis_size("doc")
    rows[...] = rows_ref[...].astype(f32)
    weight = weight_ref[...]
    embed = jnp.concatenate([rows[:, k, :] for k in range(lanes - 1)], axis=1)
    logits = lax.dot_general(
        embed.astype(bf16), weight, (((1,), (1,)), ((), ())), preferred_element_type=f32
    ) + bias_ref[...].astype(f32).reshape(1, labels)
    digits = rows[:, lanes - 1, :]
    ids = digits[:, :slots] * (PIECE * PIECE) + digits[:, slots : 2 * slots] * PIECE + digits[:, 2 * slots : 3 * slots]
    own = lax.broadcasted_iota(jnp.int32, logits.shape, 1) + (me * labels + 1)
    listed = ids.astype(jnp.int32)
    hit = own == listed[:, 0:1]
    for k in range(1, slots):
        hit = jnp.logical_or(hit, own == listed[:, k : k + 1])
    d_logit = (jax.nn.sigmoid(logits) - jnp.where(hit, 1.0, 0.0)).astype(bf16)
    part[...] = jnp.dot(d_logit, weight, preferred_element_type=f32)
    half = part.shape[0] // 2
    kind = lax.rem(me // core, 2)
    mine_ref[...] = part[pl.ds(pl.multiple_of(kind * half, half), half), :]
    other_ref[...] = part[pl.ds(pl.multiple_of((1 - kind) * half, half), half), :]


def back_kernel(seq, masks, *refs):
    grad_ref, gains_ref, weight_ref = refs[:3]
    groups = [refs[3 + 3 * g : 6 + 3 * g] for g in range(len(masks))]
    out_ref, sums_ref, own_ref, act, d_pre, saved, spreads = refs[3 + 3 * len(masks) :]
    me, core = number(), lax.axis_size("doc")
    places = [[place(me ^ m, core) for m in group] for group in masks]
    own_ref[...] = grad_ref[pl.ds(place(me, core), 1), :]
    width = gains_ref.shape[1]
    for (_, _, row_ref), group in zip(groups, places, strict=True):
        for d, at in enumerate(group):
            saved[at] = row_ref[d]
    row, normed, inverse, sums = grad_ref[...], saved[:, 0, :], saved[:, 1, :], saved[:, 2, :]
    d_normed = row * gains_ref[1:2, :]
    spread = (
        inverse
        * (
            d_normed
            - jnp.mean(d_normed, axis=-1, keepdims=True)
            - normed * jnp.mean(d_normed * normed, axis=-1, keepdims=True)
        )
        * (1.0 / seq)
    )
    spreads[...] = spread
    for (act_ref, tilt_ref, _), group in zip(groups, places, strict=True):
        for d, at in enumerate(group):
            to = pl.ds(pl.multiple_of(at * seq, seq), seq)
            act[to, :] = act_ref[d * seq : (d + 1) * seq, :]
            d_pre[to, :] = (tilt_ref[d * seq : (d + 1) * seq, :] * spreads[pl.ds(at, 1), :]).astype(bf16)
    half = 0.5 * spread
    sums_top, half_top = sums.astype(bf16), half.astype(bf16)
    sums_low = (sums - sums_top.astype(f32)).astype(bf16)
    half_low = (half - half_top.astype(f32)).astype(bf16)
    even = lax.dot_general(
        jnp.concatenate([sums_top, sums_top, sums_low], axis=0),
        jnp.concatenate([half_top, half_low, half_top], axis=0),
        (((0,), (0,)), ((), ())),
        preferred_element_type=f32,
    )
    total = even + lax.dot_general(act[...], d_pre[...], (((0,), (0,)), ((), ())), preferred_element_type=f32)
    out_ref[...] = total.astype(bf16)
    weighed = total * weight_ref[...].astype(f32)
    lanes = weighed[:, :128]
    for k in range(1, width // 128):
        lanes = lanes + weighed[:, k * 128 : (k + 1) * 128]
    sums_ref[0:1, :] = jnp.sum(lanes.T, axis=0, keepdims=True) / gains_ref[0:1, :]
    sums_ref[1:2, :] = jnp.sum(row * normed, axis=0, keepdims=True)


def final_kernel(mine_ref, other_ref, sums_ref, more_ref, weight_ref, gains_ref):
    weight_ref[...] = mine_ref[...].astype(f32) + other_ref[...].astype(f32)
    gains_ref[...] = sums_ref[...] + more_ref[...]


def final_call(mine, other, sums, more):
    rows, width = mine.shape
    steps = 4 if rows % 64 == 0 else 1
    part = pl.BlockSpec((rows // steps, width), lambda i: (i, 0))
    whole = pl.BlockSpec(sums.shape, lambda i: (0, 0))
    return pl.pallas_call(
        final_kernel,
        grid=(steps,),
        out_shape=[jax.ShapeDtypeStruct(mine.shape, f32), jax.ShapeDtypeStruct(sums.shape, f32)],
        in_specs=[part, part, whole, whole],
        out_specs=[part, whole],
        compiler_params=pltpu.CompilerParams(vmem_limit_bytes=12 << 20),
        name="final",
    )(mine, other, sums, more)


def swap(value, mask, count):
    return lax.ppermute(value, AXES, [(i, i ^ mask) for i in range(count)])


def combos(bits):
    masks = [0]
    for bit in bits:
        masks += [m | bit for m in masks]
    return masks


def gathered(tokens, norm_gains, enc_weight, head_weight, head_bias, positives):
    n_doc, count = lax.axis_size("doc"), lax.axis_size(AXES)
    seq, width = tokens.shape[1:]
    slots = positives.shape[1]
    core = n_doc
    bits = [1 << b for b in range(count.bit_length() - 1) if 1 << b != core]
    x, y, z, far = bits
    hop = functools.partial(swap, count=count)
    half, h = count // 2, seq // 2
    by_core = [i for i in range(count) if not i & core] + [i for i in range(count) if i & core]

    own = tokens.reshape(seq, width)
    held = {0: [(own, 0, seq)]}

    def exchange(plan, tied=()):
        come = {}
        for to, wanted in plan.items():
            parts = []
            for doc, low, high in wanted:
                at = 0
                for array, first, rows in held[doc]:
                    start, stop = max(low, at), min(high, at + rows)
                    if start < stop:
                        parts.append((array, first + start - at, stop - start))
                    at += rows
            come[to] = hop(parts[0][0] if not tied else join(parts, tied), to)
        new = {}
        for to, wanted in plan.items():
            at = 0
            for doc, low, high in wanted:
                new.setdefault(doc ^ to, []).append((low, come[to], at, high - low))
                at += high - low
        fresh = {}
        for doc, pieces in new.items():
            fresh[doc] = [piece[1:] for piece in sorted(pieces, key=lambda piece: piece[0])]
        held.update(fresh)
        return list(fresh), list(come.values())

    groups, masks = [], []

    def encode_held(docs):
        arrays, layout = [], []
        for doc in docs:
            pieces = []
            for array, first, rows in held[doc]:
                known = [k for k, a in enumerate(arrays) if a is array]
                if not known:
                    known = [len(arrays)]
                    arrays.append(array)
                pieces.append((known[0], first, rows))
            layout.append(pieces)
        groups.append(encode_call(arrays, layout, norm_gains, enc_weight))
        masks.append(docs)
        return groups[-1][2]

    docs_0, come_0 = exchange({x: [(0, 0, seq)], y: [(0, 0, seq)], z: [(0, 0, seq)], far: [(0, 0, seq)]})

    *group, copies = first_call(own, norm_gains, enc_weight, positives, count)
    groups.append(group)
    masks.append([0])
    rows = lax.all_to_all(copies, AXES, split_axis=0, concat_axis=0, tiled=True, axis_index_groups=[by_core])

    def cube(base):
        return {
            x: [(base | y, 0, h), (base | z, 0, h)],
            y: [(base | x, h, seq), (base | z, 0, h)],
            z: [(base | x, h, seq), (base | y, h, seq)],
        }

    def corner(base):
        return {x: [(base | y | z, 0, h)], y: [(base | x | z, h, seq)]}

    mine, other = pl.pallas_call(
        functools.partial(head_kernel, slots),
        out_shape=[jax.ShapeDtypeStruct((half, width), f32)] * 2,
        scratch_shapes=[pltpu.VMEM(rows.shape, f32), pltpu.VMEM((count, width), f32)],
        compiler_params=pltpu.CompilerParams(vmem_limit_bytes=10 << 20),
        name="head",
    )(rows, head_weight, head_bias)

    plan = cube(0)
    docs_1, _ = exchange({to: [(far, 0, seq)] + plan[to] for to in plan}, [rows])
    tied = encode_held(docs_0)
    total = add([mine, hop(other, core)])
    total = add([total] + [hop(total, m) for m in (x, y, x | y)], [tied])
    plan, last = cube(far), corner(0)
    docs_2, _ = exchange({to: plan[to] + last.get(to, []) for to in plan}, [total])
    tied = encode_held(docs_1)
    total = add([total] + [hop(total, m) for m in (z, far, z | far)], [tied])
    docs_3, _ = exchange(corner(far), [tied])
    encode_held(docs_2)
    encode_held(docs_3)

    operands = [array for group in groups for array in group]
    part, sums, row_grad = pl.pallas_call(
        functools.partial(back_kernel, seq, masks),
        out_shape=[
            jax.ShapeDtypeStruct((width, width), bf16),
            jax.ShapeDtypeStruct((2, width), f32),
            jax.ShapeDtypeStruct((1, width), f32),
        ],
        scratch_shapes=[
            pltpu.VMEM((half * seq, width), bf16),
            pltpu.VMEM((half * seq, width), bf16),
            pltpu.VMEM((half, 8, width), f32),
            pltpu.VMEM((half, width), f32),
        ],
        compiler_params=pltpu.CompilerParams(vmem_limit_bytes=32 << 20),
        name="back",
    )(total, norm_gains, enc_weight, *operands)
    weight_grad, gain_grads = final_call(part, hop(part, core), sums, hop(sums, core))
    return row_grad, weight_grad, gain_grads


def normalize(values):
    center = values - jnp.mean(values, axis=-1, keepdims=True)
    inverse = lax.rsqrt(jnp.mean(center * center, axis=-1, keepdims=True) + epsilon)
    return (center * inverse, inverse)


def encode(tok_block, gains, enc_weight):
    width = tok_block.shape[-1]
    tok_flat = tok_block.reshape(-1, width).astype(f32)
    normed_in, _ = normalize(tok_flat)
    act_in = (normed_in * gains[0]).astype(bf16)
    pre_act = jnp.dot(act_in, enc_weight, preferred_element_type=f32)
    hidden = tok_flat + jax.nn.gelu(pre_act)
    pooled = jnp.mean(hidden.reshape(tok_block.shape[0], tok_block.shape[1], width), axis=1)
    normed_out, inv_out = normalize(pooled)
    return (normed_out * gains[1], (normed_in, act_in, pre_act, normed_out, inv_out))


def encode_back(cotangent, saved, gains, enc_weight, seq_len):
    normed_in, act_in, pre_act, normed_out, inv_out = saved
    gain_out_grad = jnp.sum(cotangent * normed_out, axis=0)
    d_normed = cotangent * gains[1]
    d_pooled = inv_out * (
        d_normed
        - jnp.mean(d_normed, axis=-1, keepdims=True)
        - normed_out * jnp.mean(d_normed * normed_out, axis=-1, keepdims=True)
    )
    spread_grad = jnp.broadcast_to(
        (d_pooled / seq_len)[:, None, :], (d_pooled.shape[0], seq_len, d_pooled.shape[1])
    ).reshape(pre_act.shape)
    _, gelu_back = jax.vjp(jax.nn.gelu, pre_act)
    d_pre = gelu_back(spread_grad)[0]
    weight_grad = lax.dot_general(
        act_in.astype(f32), d_pre, (((0,), (0,)), ((), ())), precision=lax.Precision.HIGHEST, preferred_element_type=f32
    )
    d_act = lax.dot_general(
        d_pre, enc_weight.astype(f32), (((1,), (1,)), ((), ())), precision=lax.Precision.HIGHEST, preferred_element_type=f32
    )
    gain_in_grad = jnp.sum(d_act * normed_in, axis=0)
    return (weight_grad, jnp.stack([gain_in_grad, gain_out_grad]))


def head_block(embed_bf, label_lists, weight_block, bias_block, first_label):
    logits = lax.dot_general(embed_bf, weight_block, (((1,), (1,)), ((), ())), preferred_element_type=f32)
    logits = logits + bias_block.astype(f32)[None, :]
    label_ids = first_label + jnp.arange(weight_block.shape[0], dtype=jnp.int32)
    target = jnp.any(label_lists[:, :, None] == label_ids[None, None, :], axis=1).astype(f32)
    d_logit = (jax.nn.sigmoid(logits) - target).astype(bf16)
    return jnp.dot(d_logit, weight_block, preferred_element_type=f32)


def spread_out(tokens, norm_gains, enc_weight, head_weight, head_bias, positives):
    doc_count, seq_len, width = tokens.shape
    embed, saved = encode(tokens, norm_gains, enc_weight)
    col_embed, col_lists = (
        lax.all_gather(embed.astype(bf16), "label", axis=0, tiled=True),
        lax.all_gather(positives, "label", axis=0, tiled=True),
    )
    span = head_weight.shape[0] * lax.axis_size("doc")
    partial_grad = head_block(
        col_embed,
        col_lists,
        lax.all_gather(head_weight, "doc", axis=0, tiled=True),
        lax.all_gather(head_bias, "doc", axis=0, tiled=True),
        lax.axis_index("label") * span,
    )
    summed = lax.psum(partial_grad, "label")
    row_grad = lax.dynamic_slice_in_dim(summed, lax.axis_index("label") * doc_count, doc_count, 0)
    weight_part, gain_part = encode_back(row_grad, saved, norm_gains, enc_weight, seq_len)
    weight_grad, gain_grads = lax.psum((weight_part, gain_part), AXES)
    return (row_grad, weight_grad, gain_grads)


def shards(tokens, *rest):
    count = lax.axis_size(AXES)
    powers = all(size & (size - 1) == 0 for size in (count, lax.axis_size("doc")))
    fits = tokens.size * tokens.dtype.itemsize * (count // 2) <= GATHER_LIMIT
    plan = gathered if fits and powers and count == 32 and tokens.shape[0] == 1 else spread_out
    return plan(tokens, *rest)


def solution(mesh):
    placed = (
        P(AXES, None, None),
        P(),
        P(),
        P(AXES, None),
        P(AXES),
        P(AXES, None),
    )
    return jax.shard_map(
        shards,
        mesh=mesh,
        in_specs=placed,
        out_specs=(P(AXES, None), P(), P()),
        check_vma=False,
    )
```

```python
import functools
import math

import jax
import jax.numpy as jnp
from jax import lax
from jax.experimental import pallas as pl
from jax.experimental.pallas import tpu as pltpu
from jax.sharding import PartitionSpec as P

epsilon = 1e-05
AXES = ("label", "doc")
PIECE_BITS = 8
PIECE = 1 << PIECE_BITS
DIGITS = 3
GATHER_LIMIT = 8 << 20
FIRST_LIMIT = 10 << 20
f32, bf16 = jnp.float32, jnp.bfloat16


def encode_rows(tok, gains, weight):
    values = tok.astype(f32)
    center = values - jnp.mean(values, axis=-1, keepdims=True)
    inverse = lax.rsqrt(jnp.mean(center * center, axis=-1, keepdims=True) + epsilon)
    act = (center * inverse * gains[0:1]).astype(bf16)
    pre = jnp.dot(act, weight, preferred_element_type=f32)
    scale = math.sqrt(2.0 / math.pi)
    square = pre * pre
    bend = jnp.tanh(pre * (scale + (scale * 0.044715) * square))
    half = 0.5 * pre
    bent = half * bend
    tilt = 0.5 * bend + (half - bent * bend) * (scale + (3.0 * scale * 0.044715) * square)
    total = jnp.sum(values + (half + bent), axis=0, keepdims=True)
    return act, tilt, total, jnp.sum(act.astype(f32), axis=0, keepdims=True)


def norm_row(pooled):
    center = pooled - jnp.mean(pooled, axis=-1, keepdims=True)
    inverse = lax.rsqrt(jnp.mean(center * center, axis=-1, keepdims=True) + epsilon)
    return center * inverse, inverse


def place(device, core):
    return (device // (2 * core)) * core + device % core


def number():
    return lax.axis_index("label") * lax.axis_size("doc") + lax.axis_index("doc")


def encode_into(layout, toks, gains, weight, act_ref, tilt_ref, row_ref):
    at = 0
    for d, doc in enumerate(layout):
        seq = sum(rows for _, _, rows in doc)
        total, acts = 0.0, 0.0
        for operand, first, rows in doc:
            for start in range(0, rows, seq // 2):
                span = min(seq // 2, rows)
                tok = toks[operand][first + start : first + start + span, :]
                act, tilt, part, sums = encode_rows(tok, gains, weight)
                act_ref[at : at + span, :] = act
                tilt_ref[at : at + span, :] = tilt
                total, acts, at = total + part, acts + sums, at + span
        normed, inverse = norm_row(total * (1.0 / seq))
        row_ref[d, 0:1, :] = normed
        row_ref[d, 1:2, :] = jnp.broadcast_to(inverse, normed.shape)
        row_ref[d, 2:3, :] = acts
    return normed


def first_kernel(*refs):
    sources, (act_ref, tilt_ref, row_ref, embed_ref), held, (digits, sems) = refs[:4], refs[4:8], refs[8:12], refs[12:]
    copies = [pltpu.make_async_copy(a, b, sems.at[k]) for k, (a, b) in enumerate(zip(sources, held, strict=True))]
    for copy in copies:
        copy.start()
    for copy in copies:
        copy.wait()
    tok, gains_ref, weight_ref, listed_ref = held
    gains = gains_ref[...]
    seq, width = tok.shape
    slots = listed_ref.shape[1]
    normed = encode_into([[(0, 0, seq)]], [tok], gains, weight_ref[...], act_ref, tilt_ref, row_ref)
    embed = normed * gains[1:2]
    digits[...] = jnp.zeros_like(digits)
    shifted = listed_ref[...] + 1
    for k in range(DIGITS):
        digit = jnp.bitwise_and(jnp.right_shift(shifted, PIECE_BITS * (DIGITS - 1 - k)), PIECE - 1)
        digits[:, k * slots : (k + 1) * slots] = digit.astype(f32)
    lanes = [embed[:, k * 128 : (k + 1) * 128] for k in range(width // 128)] + [digits[...]]
    lanes += [jnp.zeros((1, 128), f32)] * (embed_ref.shape[1] - len(lanes))
    block = jnp.concatenate(lanes, axis=0).astype(bf16)
    embed_ref[...] = jnp.broadcast_to(block[None], embed_ref.shape)


def encode_kernel(layout, *refs):
    toks, (gains_ref, weight_ref, act_ref, tilt_ref, row_ref) = refs[:-5], refs[-5:]
    encode_into(layout, toks, gains_ref[...], weight_ref[...], act_ref, tilt_ref, row_ref)


def encode_shapes(rows, docs, width):
    return [
        jax.ShapeDtypeStruct((rows, width), bf16),
        jax.ShapeDtypeStruct((rows, width), f32),
        jax.ShapeDtypeStruct((docs, 8, width), f32),
    ]


def first_call(own, gains, weight, listed, copies):
    seq, width = own.shape
    sources = [own, gains, weight, listed]
    deep = -(-(width // 128 + 1) // 8) * 8
    return pl.pallas_call(
        first_kernel,
        out_shape=encode_shapes(seq, 1, width) + [jax.ShapeDtypeStruct((copies, deep, 128), bf16)],
        in_specs=[pl.BlockSpec(memory_space=pltpu.HBM)] * 4,
        scratch_shapes=[pltpu.VMEM(a.shape, a.dtype) for a in sources]
        + [pltpu.VMEM((1, 128), f32), pltpu.SemaphoreType.DMA((4,))],
        compiler_params=pltpu.CompilerParams(vmem_limit_bytes=FIRST_LIMIT),
        name="first",
    )(*sources)


def encode_call(arrays, layout, gains, weight):
    rows = sum(piece[2] for doc in layout for piece in doc)
    return pl.pallas_call(
        functools.partial(encode_kernel, layout),
        out_shape=encode_shapes(rows, len(layout), gains.shape[1]),
        compiler_params=pltpu.CompilerParams(vmem_limit_bytes=14 << 20),
        name="encode",
    )(*arrays, gains, weight)


def join_kernel(pieces, *refs):
    out_ref = refs[-1]
    at = 0
    for operand, first, rows in pieces:
        out_ref[at : at + rows, :] = refs[operand][first : first + rows, :]
        at += rows


def join(parts, tied=()):
    arrays, pieces = [], []
    for array, first, rows in parts:
        known = [k for k, a in enumerate(arrays) if a is array]
        if not known:
            known = [len(arrays)]
            arrays.append(array)
        pieces.append((known[0], first, rows))
    vmem, anywhere = pl.BlockSpec(memory_space=pltpu.VMEM), pl.BlockSpec(memory_space=pl.ANY)
    return pl.pallas_call(
        functools.partial(join_kernel, pieces),
        out_shape=jax.ShapeDtypeStruct((sum(p[2] for p in pieces), arrays[0].shape[1]), arrays[0].dtype),
        in_specs=[vmem] * len(arrays) + [anywhere] * len(tied),
        compiler_params=pltpu.CompilerParams(vmem_limit_bytes=4 << 20),
        name="join",
    )(*arrays, *tied)


def add_kernel(count, *refs):
    parts = [ref[...] for ref in refs[:count]]
    while len(parts) > 1:
        parts = [parts[i] + parts[i + 1] for i in range(0, len(parts), 2)]
    refs[-1][...] = parts[0]


def add(parts, tied=()):
    vmem, anywhere = pl.BlockSpec(memory_space=pltpu.VMEM), pl.BlockSpec(memory_space=pl.ANY)
    return pl.pallas_call(
        functools.partial(add_kernel, len(parts)),
        out_shape=jax.ShapeDtypeStruct(parts[0].shape, parts[0].dtype),
        in_specs=[vmem] * len(parts) + [anywhere] * len(tied),
        compiler_params=pltpu.CompilerParams(vmem_limit_bytes=4 << 20),
        name="add",
    )(*parts, *tied)


def mark_kernel(*refs):
    refs[-1][...] = jnp.zeros_like(refs[-1])


def mark(arrays):
    return pl.pallas_call(
        mark_kernel,
        out_shape=jax.ShapeDtypeStruct((8, 128), f32),
        in_specs=[pl.BlockSpec(memory_space=pl.ANY)] * len(arrays),
        compiler_params=pltpu.CompilerParams(vmem_limit_bytes=1 << 20),
        name="mark",
    )(*arrays)


def head_kernel(slots, rows_ref, weight_ref, bias_ref, mine_ref, other_ref, rows, part):
    labels, width = weight_ref.shape
    lanes = width // 128 + 1
    me, core = number(), lax.axis_size("doc")
    rows[...] = rows_ref[...].astype(f32)
    weight = weight_ref[...]
    embed = jnp.concatenate([rows[:, k, :] for k in range(lanes - 1)], axis=1)
    logits = lax.dot_general(
        embed.astype(bf16), weight, (((1,), (1,)), ((), ())), preferred_element_type=f32
    ) + bias_ref[...].astype(f32).reshape(1, labels)
    digits = rows[:, lanes - 1, :]
    ids = digits[:, :slots] * (PIECE * PIECE) + digits[:, slots : 2 * slots] * PIECE + digits[:, 2 * slots : 3 * slots]
    own = lax.broadcasted_iota(jnp.int32, logits.shape, 1) + (me * labels + 1)
    listed = ids.astype(jnp.int32)
    hit = own == listed[:, 0:1]
    for k in range(1, slots):
        hit = jnp.logical_or(hit, own == listed[:, k : k + 1])
    d_logit = (jax.nn.sigmoid(logits) - jnp.where(hit, 1.0, 0.0)).astype(bf16)
    part[...] = jnp.dot(d_logit, weight, preferred_element_type=f32)
    half = part.shape[0] // 2
    kind = lax.rem(me // core, 2)
    mine_ref[...] = part[pl.ds(pl.multiple_of(kind * half, half), half), :]
    other_ref[...] = part[pl.ds(pl.multiple_of((1 - kind) * half, half), half), :]


def back_kernel(seq, masks, *refs):
    grad_ref, gains_ref, weight_ref = refs[:3]
    groups = [refs[3 + 3 * g : 6 + 3 * g] for g in range(len(masks))]
    out_ref, own_ref, act, d_pre, saved, spreads = refs[3 + 3 * len(masks) :]
    me, core = number(), lax.axis_size("doc")
    places = [[place(me ^ m, core) for m in group] for group in masks]
    own_ref[...] = grad_ref[pl.ds(place(me, core), 1), :]
    width = gains_ref.shape[1]
    for (_, _, row_ref), group in zip(groups, places, strict=True):
        for d, at in enumerate(group):
            saved[at] = row_ref[d]
    row, normed, inverse, sums = grad_ref[...], saved[:, 0, :], saved[:, 1, :], saved[:, 2, :]
    d_normed = row * gains_ref[1:2, :]
    spread = (
        inverse
        * (
            d_normed
            - jnp.mean(d_normed, axis=-1, keepdims=True)
            - normed * jnp.mean(d_normed * normed, axis=-1, keepdims=True)
        )
        * (1.0 / seq)
    )
    spreads[...] = spread
    for (act_ref, tilt_ref, _), group in zip(groups, places, strict=True):
        for d, at in enumerate(group):
            to = pl.ds(pl.multiple_of(at * seq, seq), seq)
            act[to, :] = act_ref[d * seq : (d + 1) * seq, :]
            d_pre[to, :] = (tilt_ref[d * seq : (d + 1) * seq, :] * spreads[pl.ds(at, 1), :]).astype(bf16)
    even = 0.5 * spread
    sums_top, half_top = sums.astype(bf16), even.astype(bf16)
    sums_low = (sums - sums_top.astype(f32)).astype(bf16)
    half_low = (even - half_top.astype(f32)).astype(bf16)
    even = lax.dot_general(
        jnp.concatenate([sums_top, sums_top, sums_low], axis=0),
        jnp.concatenate([half_top, half_low, half_top], axis=0),
        (((0,), (0,)), ((), ())),
        preferred_element_type=f32,
    )
    total = even + lax.dot_general(act[...], d_pre[...], (((0,), (0,)), ((), ())), preferred_element_type=f32)
    out_ref[:width, :] = total.astype(bf16)
    weighed = total * weight_ref[...].astype(f32)
    lanes = weighed[:, :128]
    for k in range(1, width // 128):
        lanes = lanes + weighed[:, k * 128 : (k + 1) * 128]
    gain_in = jnp.sum(lanes.T, axis=0, keepdims=True) / gains_ref[0:1, :]
    gain_out = jnp.sum(row * normed, axis=0, keepdims=True)
    rest, terms = jnp.concatenate([gain_in, gain_out], axis=0), []
    for _ in range(3):
        terms.append(rest.astype(bf16).astype(f32))
        rest = rest - terms[-1]
    terms.append(jnp.zeros((16 - 2 * len(terms), width), f32))
    out_ref[width:, :] = jnp.concatenate(terms, axis=0).astype(bf16)


def final_kernel(steps, mine_ref, other_ref, weight_ref, gains_ref, total, sems):
    rows = weight_ref.shape[0]
    span = rows // steps
    copies = []
    for k in range(steps):
        part = pl.ds(k * span, span)
        total[part, :] = mine_ref[part, :].astype(f32) + other_ref[part, :].astype(f32)
        copies.append(pltpu.make_async_copy(total.at[part, :], weight_ref.at[part, :], sems.at[k]))
        copies[-1].start()
    mine, other = mine_ref[rows:, :].astype(f32), other_ref[rows:, :].astype(f32)
    gains_ref[...] = (mine[0:2] + mine[2:4] + mine[4:6]) + (other[0:2] + other[2:4] + other[4:6])
    for copy in copies:
        copy.wait()


def final_call(mine, other):
    width = mine.shape[1]
    steps = 8 if width % 128 == 0 else 1
    vmem, hbm = pl.BlockSpec(memory_space=pltpu.VMEM), pl.BlockSpec(memory_space=pltpu.HBM)
    return pl.pallas_call(
        functools.partial(final_kernel, steps),
        out_shape=[jax.ShapeDtypeStruct((width, width), f32), jax.ShapeDtypeStruct((2, width), f32)],
        in_specs=[vmem] * 2,
        out_specs=[hbm, vmem],
        scratch_shapes=[pltpu.VMEM((width, width), f32), pltpu.SemaphoreType.DMA((steps,))],
        compiler_params=pltpu.CompilerParams(vmem_limit_bytes=12 << 20),
        name="final",
    )(mine, other)


def swap(value, mask, count):
    return lax.ppermute(value, AXES, [(i, i ^ mask) for i in range(count)])


def combos(bits):
    masks = [0]
    for bit in bits:
        masks += [m | bit for m in masks]
    return masks


def gathered(tokens, norm_gains, enc_weight, head_weight, head_bias, positives):
    n_doc, count = lax.axis_size("doc"), lax.axis_size(AXES)
    seq, width = tokens.shape[1:]
    slots = positives.shape[1]
    core = n_doc
    bits = [1 << b for b in range(count.bit_length() - 1) if 1 << b != core]
    x, y, z, far = bits
    hop = functools.partial(swap, count=count)
    half, h = count // 2, seq // 2
    by_core = [i for i in range(count) if not i & core] + [i for i in range(count) if i & core]

    own = tokens.reshape(seq, width)
    held = {0: [(own, 0, seq)]}

    def exchange(plan, tied=()):
        come = {}
        for to, wanted in plan.items():
            parts = []
            for doc, low, high in wanted:
                at = 0
                for array, first, rows in held[doc]:
                    start, stop = max(low, at), min(high, at + rows)
                    if start < stop:
                        parts.append((array, first + start - at, stop - start))
                    at += rows
            come[to] = hop(parts[0][0] if not tied else join(parts, tied), to)
        new = {}
        for to, wanted in plan.items():
            at = 0
            for doc, low, high in wanted:
                new.setdefault(doc ^ to, []).append((low, come[to], at, high - low))
                at += high - low
        fresh = {}
        for doc, pieces in new.items():
            fresh[doc] = [piece[1:] for piece in sorted(pieces, key=lambda piece: piece[0])]
        held.update(fresh)
        return list(fresh), list(come.values())

    groups, masks = [], []

    def encode_held(docs):
        arrays, layout = [], []
        for doc in docs:
            pieces = []
            for array, first, rows in held[doc]:
                known = [k for k, a in enumerate(arrays) if a is array]
                if not known:
                    known = [len(arrays)]
                    arrays.append(array)
                pieces.append((known[0], first, rows))
            layout.append(pieces)
        groups.append(encode_call(arrays, layout, norm_gains, enc_weight))
        masks.append(docs)
        return groups[-1][2]

    whole = (0, 0, seq)
    docs_0, _ = exchange({far: [whole], z: [whole], x: [whole], y: [whole]})
    *group, copies = first_call(own, norm_gains, enc_weight, positives, count)
    groups.append(group)
    masks.append([0])
    rows = lax.all_to_all(copies, AXES, split_axis=0, concat_axis=0, tiled=True, axis_index_groups=[by_core])

    def spread(full, corners):
        wanted = [(doc, 0, seq) for doc in full]
        return {
            x: wanted + [(y | doc, 0, h) for doc in corners],
            y: wanted + [(x | doc, h, seq) for doc in corners],
        }

    early = mark([held[far][0][0]])
    plan = spread([z, far], [0])
    plan[z] = [(far, 0, seq)]
    docs_1, _ = exchange(plan, [groups[0][2], early])
    mine, other = pl.pallas_call(
        functools.partial(head_kernel, slots),
        out_shape=[jax.ShapeDtypeStruct((half, width), f32)] * 2,
        scratch_shapes=[pltpu.VMEM(rows.shape, f32), pltpu.VMEM((count, width), f32)],
        compiler_params=pltpu.CompilerParams(vmem_limit_bytes=10 << 20),
        name="head",
    )(rows, head_weight, head_bias)

    total = add([mine, hop(other, core)])
    plan = spread([z | far], [z, far])
    docs_2, _ = exchange(plan, [total])
    tied = encode_held(docs_0)
    total = add([total, hop(total, z)], [tied])
    tied = encode_held(docs_1[:4])
    total = add([total, hop(total, far)], [tied])
    plan = spread([], [z | far])
    docs_3, _ = exchange(plan, [total])
    rest = docs_1[4:]
    tied = [encode_held(rest)] if rest else []
    total = add([total, hop(total, x)], tied)
    tied = encode_held(docs_2)
    total = add([total, hop(total, y)], [tied])
    encode_held(docs_3)

    operands = [array for group in groups for array in group]
    part, row_grad = pl.pallas_call(
        functools.partial(back_kernel, seq, masks),
        out_shape=[
            jax.ShapeDtypeStruct((width + 16, width), bf16),
            jax.ShapeDtypeStruct((1, width), f32),
        ],
        scratch_shapes=[
            pltpu.VMEM((half * seq, width), bf16),
            pltpu.VMEM((half * seq, width), bf16),
            pltpu.VMEM((half, 8, width), f32),
            pltpu.VMEM((half, width), f32),
        ],
        compiler_params=pltpu.CompilerParams(vmem_limit_bytes=32 << 20),
        name="back",
    )(total, norm_gains, enc_weight, *operands)
    weight_grad, gain_grads = final_call(part, hop(part, core))
    return row_grad, weight_grad, gain_grads


def normalize(values):
    center = values - jnp.mean(values, axis=-1, keepdims=True)
    inverse = lax.rsqrt(jnp.mean(center * center, axis=-1, keepdims=True) + epsilon)
    return (center * inverse, inverse)


def encode(tok_block, gains, enc_weight):
    width = tok_block.shape[-1]
    tok_flat = tok_block.reshape(-1, width).astype(f32)
    normed_in, _ = normalize(tok_flat)
    act_in = (normed_in * gains[0]).astype(bf16)
    pre_act = jnp.dot(act_in, enc_weight, preferred_element_type=f32)
    hidden = tok_flat + jax.nn.gelu(pre_act)
    pooled = jnp.mean(hidden.reshape(tok_block.shape[0], tok_block.shape[1], width), axis=1)
    normed_out, inv_out = normalize(pooled)
    return (normed_out * gains[1], (normed_in, act_in, pre_act, normed_out, inv_out))


def encode_back(cotangent, saved, gains, enc_weight, seq_len):
    normed_in, act_in, pre_act, normed_out, inv_out = saved
    gain_out_grad = jnp.sum(cotangent * normed_out, axis=0)
    d_normed = cotangent * gains[1]
    d_pooled = inv_out * (
        d_normed
        - jnp.mean(d_normed, axis=-1, keepdims=True)
        - normed_out * jnp.mean(d_normed * normed_out, axis=-1, keepdims=True)
    )
    spread_grad = jnp.broadcast_to(
        (d_pooled / seq_len)[:, None, :], (d_pooled.shape[0], seq_len, d_pooled.shape[1])
    ).reshape(pre_act.shape)
    _, gelu_back = jax.vjp(jax.nn.gelu, pre_act)
    d_pre = gelu_back(spread_grad)[0]
    weight_grad = lax.dot_general(
        act_in.astype(f32), d_pre, (((0,), (0,)), ((), ())), precision=lax.Precision.HIGHEST, preferred_element_type=f32
    )
    d_act = lax.dot_general(
        d_pre, enc_weight.astype(f32), (((1,), (1,)), ((), ())), precision=lax.Precision.HIGHEST, preferred_element_type=f32
    )
    gain_in_grad = jnp.sum(d_act * normed_in, axis=0)
    return (weight_grad, jnp.stack([gain_in_grad, gain_out_grad]))


def head_block(embed_bf, label_lists, weight_block, bias_block, first_label):
    logits = lax.dot_general(embed_bf, weight_block, (((1,), (1,)), ((), ())), preferred_element_type=f32)
    logits = logits + bias_block.astype(f32)[None, :]
    label_ids = first_label + jnp.arange(weight_block.shape[0], dtype=jnp.int32)
    target = jnp.any(label_lists[:, :, None] == label_ids[None, None, :], axis=1).astype(f32)
    d_logit = (jax.nn.sigmoid(logits) - target).astype(bf16)
    return jnp.dot(d_logit, weight_block, preferred_element_type=f32)


def spread_out(tokens, norm_gains, enc_weight, head_weight, head_bias, positives):
    doc_count, seq_len, width = tokens.shape
    embed, saved = encode(tokens, norm_gains, enc_weight)
    col_embed, col_lists = (
        lax.all_gather(embed.astype(bf16), "label", axis=0, tiled=True),
        lax.all_gather(positives, "label", axis=0, tiled=True),
    )
    span = head_weight.shape[0] * lax.axis_size("doc")
    partial_grad = head_block(
        col_embed,
        col_lists,
        lax.all_gather(head_weight, "doc", axis=0, tiled=True),
        lax.all_gather(head_bias, "doc", axis=0, tiled=True),
        lax.axis_index("label") * span,
    )
    summed = lax.psum(partial_grad, "label")
    row_grad = lax.dynamic_slice_in_dim(summed, lax.axis_index("label") * doc_count, doc_count, 0)
    weight_part, gain_part = encode_back(row_grad, saved, norm_gains, enc_weight, seq_len)
    weight_grad, gain_grads = lax.psum((weight_part, gain_part), AXES)
    return (row_grad, weight_grad, gain_grads)


def shards(tokens, *rest):
    count = lax.axis_size(AXES)
    powers = all(size & (size - 1) == 0 for size in (count, lax.axis_size("doc")))
    fits = tokens.size * tokens.dtype.itemsize * (count // 2) <= GATHER_LIMIT
    plan = gathered if fits and powers and count == 32 and tokens.shape[0] == 1 else spread_out
    return plan(tokens, *rest)


def solution(mesh):
    placed = (
        P(AXES, None, None),
        P(),
        P(),
        P(AXES, None),
        P(AXES),
        P(AXES, None),
    )
    return jax.shard_map(
        shards,
        mesh=mesh,
        in_specs=placed,
        out_specs=(P(AXES, None), P(), P()),
        check_vma=False,
    )
```

```python
import functools
import math

import jax
import jax.numpy as jnp
from jax import lax
from jax.experimental import pallas as pl
from jax.experimental.pallas import tpu as pltpu
from jax.sharding import PartitionSpec as P

epsilon = 1e-05
AXES = ("label", "doc")
PIECE_BITS = 8
PIECE = 1 << PIECE_BITS
DIGITS = 3
GATHER_LIMIT = 8 << 20
FIRST_LIMIT = 10 << 20
f32, bf16 = jnp.float32, jnp.bfloat16


def enter(tok, gains):
    values = tok.astype(f32)
    center = values - jnp.mean(values, axis=-1, keepdims=True)
    inverse = lax.rsqrt(jnp.mean(center * center, axis=-1, keepdims=True) + epsilon)
    act = (center * inverse * gains[0:1]).astype(bf16)
    return act, jnp.sum(act.astype(f32), axis=0, keepdims=True)


def bend(tok, pre):
    scale = math.sqrt(2.0 / math.pi)
    square = pre * pre
    half = 0.5 * jnp.tanh(pre * (scale + (scale * 0.044715) * square))
    gelu = pre * (0.5 + half)
    tilt = half + gelu * (0.5 - half) * (2.0 * scale + (6.0 * scale * 0.044715) * square)
    return tilt, jnp.sum(tok.astype(f32) + gelu, axis=0, keepdims=True)


def norm_row(pooled):
    center = pooled - jnp.mean(pooled, axis=-1, keepdims=True)
    inverse = lax.rsqrt(jnp.mean(center * center, axis=-1, keepdims=True) + epsilon)
    return center * inverse, inverse


def place(device, core):
    return (device // (2 * core)) * core + device % core


def number():
    return lax.axis_index("label") * lax.axis_size("doc") + lax.axis_index("doc")


def encode_into(layout, toks, gains, weight, act_ref, tilt_ref, row_ref):
    seq = sum(rows for _, _, rows in layout[0])
    span = seq // 2
    halves = []
    for doc in layout:
        for operand, first, rows in doc:
            halves += [(operand, first + start) for start in range(0, rows, span)]
    acts = []
    for k, (operand, first) in enumerate(halves):
        act, sums = enter(toks[operand][first : first + span, :], gains)
        act_ref[k * span : (k + 1) * span, :] = act
        acts.append(sums)
    totals = []
    for k, (operand, first) in enumerate(halves):
        if k % 2 == 0:
            pre = jnp.dot(act_ref[k * span : (k + 2) * span, :], weight, preferred_element_type=f32)
        tilt, sums = bend(toks[operand][first : first + span, :], pre[k % 2 * span : (k % 2 + 1) * span])
        tilt_ref[k * span : (k + 1) * span, :] = tilt
        totals.append(sums)
    for d in range(len(layout)):
        normed, inverse = norm_row((totals[2 * d] + totals[2 * d + 1]) * (1.0 / seq))
        row_ref[d, 0:1, :] = normed
        row_ref[d, 1:2, :] = jnp.broadcast_to(inverse, normed.shape)
        row_ref[d, 2:3, :] = acts[2 * d] + acts[2 * d + 1]
    return normed


def first_kernel(*refs):
    sources, (act_ref, tilt_ref, row_ref, embed_ref), held, (digits, sems) = refs[:4], refs[4:8], refs[8:12], refs[12:]
    copies = [pltpu.make_async_copy(a, b, sems.at[k]) for k, (a, b) in enumerate(zip(sources, held, strict=True))]
    for copy in copies:
        copy.start()
    for copy in copies:
        copy.wait()
    tok, gains_ref, weight_ref, listed_ref = held
    gains = gains_ref[...]
    seq, width = tok.shape
    slots = listed_ref.shape[1]
    normed = encode_into([[(0, 0, seq)]], [tok], gains, weight_ref[...], act_ref, tilt_ref, row_ref)
    embed = normed * gains[1:2]
    digits[...] = jnp.zeros_like(digits)
    shifted = listed_ref[...] + 1
    for k in range(DIGITS):
        digit = jnp.bitwise_and(jnp.right_shift(shifted, PIECE_BITS * (DIGITS - 1 - k)), PIECE - 1)
        digits[:, k * slots : (k + 1) * slots] = digit.astype(f32)
    lanes = [embed[:, k * 128 : (k + 1) * 128] for k in range(width // 128)] + [digits[...]]
    lanes += [jnp.zeros((1, 128), f32)] * (embed_ref.shape[1] - len(lanes))
    block = jnp.concatenate(lanes, axis=0).astype(bf16)
    embed_ref[...] = jnp.broadcast_to(block[None], embed_ref.shape)


def encode_kernel(layout, *refs):
    toks, (gains_ref, weight_ref, act_ref, tilt_ref, row_ref) = refs[:-5], refs[-5:]
    encode_into(layout, toks, gains_ref[...], weight_ref[...], act_ref, tilt_ref, row_ref)


def encode_shapes(rows, docs, width):
    return [
        jax.ShapeDtypeStruct((rows, width), bf16),
        jax.ShapeDtypeStruct((rows, width), f32),
        jax.ShapeDtypeStruct((docs, 8, width), f32),
    ]


def first_call(own, gains, weight, listed, copies):
    seq, width = own.shape
    sources = [own, gains, weight, listed]
    deep = -(-(width // 128 + 1) // 8) * 8
    return pl.pallas_call(
        first_kernel,
        out_shape=encode_shapes(seq, 1, width) + [jax.ShapeDtypeStruct((copies, deep, 128), bf16)],
        in_specs=[pl.BlockSpec(memory_space=pltpu.HBM)] * 4,
        scratch_shapes=[pltpu.VMEM(a.shape, a.dtype) for a in sources]
        + [pltpu.VMEM((1, 128), f32), pltpu.SemaphoreType.DMA((4,))],
        compiler_params=pltpu.CompilerParams(vmem_limit_bytes=FIRST_LIMIT),
        name="first",
    )(*sources)


def encode_call(arrays, layout, gains, weight):
    rows = sum(piece[2] for doc in layout for piece in doc)
    return pl.pallas_call(
        functools.partial(encode_kernel, layout),
        out_shape=encode_shapes(rows, len(layout), gains.shape[1]),
        compiler_params=pltpu.CompilerParams(vmem_limit_bytes=14 << 20),
        name="encode",
    )(*arrays, gains, weight)


def join_kernel(pieces, *refs):
    out_ref = refs[-1]
    at = 0
    for operand, first, rows in pieces:
        out_ref[at : at + rows, :] = refs[operand][first : first + rows, :]
        at += rows


def join(parts, tied=()):
    arrays, pieces = [], []
    for array, first, rows in parts:
        known = [k for k, a in enumerate(arrays) if a is array]
        if not known:
            known = [len(arrays)]
            arrays.append(array)
        pieces.append((known[0], first, rows))
    vmem, anywhere = pl.BlockSpec(memory_space=pltpu.VMEM), pl.BlockSpec(memory_space=pl.ANY)
    return pl.pallas_call(
        functools.partial(join_kernel, pieces),
        out_shape=jax.ShapeDtypeStruct((sum(p[2] for p in pieces), arrays[0].shape[1]), arrays[0].dtype),
        in_specs=[vmem] * len(arrays) + [anywhere] * len(tied),
        compiler_params=pltpu.CompilerParams(vmem_limit_bytes=4 << 20),
        name="join",
    )(*arrays, *tied)


def add_kernel(count, *refs):
    parts = [ref[...] for ref in refs[:count]]
    while len(parts) > 1:
        parts = [parts[i] + parts[i + 1] for i in range(0, len(parts), 2)]
    refs[-1][...] = parts[0]


def add(parts, tied=()):
    vmem, anywhere = pl.BlockSpec(memory_space=pltpu.VMEM), pl.BlockSpec(memory_space=pl.ANY)
    return pl.pallas_call(
        functools.partial(add_kernel, len(parts)),
        out_shape=jax.ShapeDtypeStruct(parts[0].shape, parts[0].dtype),
        in_specs=[vmem] * len(parts) + [anywhere] * len(tied),
        compiler_params=pltpu.CompilerParams(vmem_limit_bytes=4 << 20),
        name="add",
    )(*parts, *tied)


def mark_kernel(*refs):
    refs[-1][...] = jnp.zeros_like(refs[-1])


def mark(arrays):
    return pl.pallas_call(
        mark_kernel,
        out_shape=jax.ShapeDtypeStruct((8, 128), f32),
        in_specs=[pl.BlockSpec(memory_space=pl.ANY)] * len(arrays),
        compiler_params=pltpu.CompilerParams(vmem_limit_bytes=1 << 20),
        name="mark",
    )(*arrays)


def head_kernel(slots, rows_ref, weight_ref, bias_ref, mine_ref, other_ref, rows, part):
    labels, width = weight_ref.shape
    lanes = width // 128 + 1
    me, core = number(), lax.axis_size("doc")
    rows[...] = rows_ref[...].astype(f32)
    weight = weight_ref[...]
    embed = jnp.concatenate([rows[:, k, :] for k in range(lanes - 1)], axis=1)
    logits = lax.dot_general(
        embed.astype(bf16), weight, (((1,), (1,)), ((), ())), preferred_element_type=f32
    ) + bias_ref[...].astype(f32).reshape(1, labels)
    digits = rows[:, lanes - 1, :]
    ids = digits[:, :slots] * (PIECE * PIECE) + digits[:, slots : 2 * slots] * PIECE + digits[:, 2 * slots : 3 * slots]
    own = lax.broadcasted_iota(jnp.int32, logits.shape, 1) + (me * labels + 1)
    listed = ids.astype(jnp.int32)
    hit = own == listed[:, 0:1]
    for k in range(1, slots):
        hit = jnp.logical_or(hit, own == listed[:, k : k + 1])
    d_logit = (jax.nn.sigmoid(logits) - jnp.where(hit, 1.0, 0.0)).astype(bf16)
    part[...] = jnp.dot(d_logit, weight, preferred_element_type=f32)
    half = part.shape[0] // 2
    kind = lax.rem(me // core, 2)
    mine_ref[...] = part[pl.ds(pl.multiple_of(kind * half, half), half), :]
    other_ref[...] = part[pl.ds(pl.multiple_of((1 - kind) * half, half), half), :]


def back_kernel(seq, masks, *refs):
    grad_ref, gains_ref, weight_ref = refs[:3]
    groups = [refs[3 + 3 * g : 6 + 3 * g] for g in range(len(masks))]
    out_ref, own_ref, act, d_pre, saved, spreads = refs[3 + 3 * len(masks) :]
    me, core = number(), lax.axis_size("doc")
    places = [[place(me ^ m, core) for m in group] for group in masks]
    own_ref[...] = grad_ref[pl.ds(place(me, core), 1), :]
    width = gains_ref.shape[1]
    for (_, _, row_ref), group in zip(groups, places, strict=True):
        for d, at in enumerate(group):
            saved[at] = row_ref[d]
    row, normed, inverse, sums = grad_ref[...], saved[:, 0, :], saved[:, 1, :], saved[:, 2, :]
    d_normed = row * gains_ref[1:2, :]
    spread = (
        inverse
        * (
            d_normed
            - jnp.mean(d_normed, axis=-1, keepdims=True)
            - normed * jnp.mean(d_normed * normed, axis=-1, keepdims=True)
        )
        * (1.0 / seq)
    )
    spreads[...] = spread
    for (act_ref, tilt_ref, _), group in zip(groups, places, strict=True):
        for d, at in enumerate(group):
            to = pl.ds(pl.multiple_of(at * seq, seq), seq)
            act[to, :] = act_ref[d * seq : (d + 1) * seq, :]
            d_pre[to, :] = (tilt_ref[d * seq : (d + 1) * seq, :] * spreads[pl.ds(at, 1), :]).astype(bf16)
    even = 0.5 * spread
    sums_top, half_top = sums.astype(bf16), even.astype(bf16)
    sums_low = (sums - sums_top.astype(f32)).astype(bf16)
    half_low = (even - half_top.astype(f32)).astype(bf16)
    even = lax.dot_general(
        jnp.concatenate([sums_top, sums_top, sums_low], axis=0),
        jnp.concatenate([half_top, half_low, half_top], axis=0),
        (((0,), (0,)), ((), ())),
        preferred_element_type=f32,
    )
    total = even + lax.dot_general(act[...], d_pre[...], (((0,), (0,)), ((), ())), preferred_element_type=f32)
    out_ref[:width, :] = total.astype(bf16)
    weighed = total * weight_ref[...].astype(f32)
    lanes = weighed[:, :128]
    for k in range(1, width // 128):
        lanes = lanes + weighed[:, k * 128 : (k + 1) * 128]
    gain_in = jnp.sum(lanes.T, axis=0, keepdims=True) / gains_ref[0:1, :]
    gain_out = jnp.sum(row * normed, axis=0, keepdims=True)
    rest, terms = jnp.concatenate([gain_in, gain_out], axis=0), []
    for _ in range(3):
        terms.append(rest.astype(bf16).astype(f32))
        rest = rest - terms[-1]
    terms.append(jnp.zeros((16 - 2 * len(terms), width), f32))
    out_ref[width:, :] = jnp.concatenate(terms, axis=0).astype(bf16)


def final_kernel(steps, mine_ref, other_ref, weight_ref, gains_ref, total, sems):
    rows = weight_ref.shape[0]
    span = rows // steps
    copies = []
    for k in range(steps):
        part = pl.ds(k * span, span)
        total[part, :] = mine_ref[part, :].astype(f32) + other_ref[part, :].astype(f32)
        copies.append(pltpu.make_async_copy(total.at[part, :], weight_ref.at[part, :], sems.at[k]))
        copies[-1].start()
    mine, other = mine_ref[rows:, :].astype(f32), other_ref[rows:, :].astype(f32)
    gains_ref[...] = (mine[0:2] + mine[2:4] + mine[4:6]) + (other[0:2] + other[2:4] + other[4:6])
    for copy in copies:
        copy.wait()


def final_call(mine, other):
    width = mine.shape[1]
    steps = 8 if width % 128 == 0 else 1
    vmem, hbm = pl.BlockSpec(memory_space=pltpu.VMEM), pl.BlockSpec(memory_space=pltpu.HBM)
    return pl.pallas_call(
        functools.partial(final_kernel, steps),
        out_shape=[jax.ShapeDtypeStruct((width, width), f32), jax.ShapeDtypeStruct((2, width), f32)],
        in_specs=[vmem] * 2,
        out_specs=[hbm, vmem],
        scratch_shapes=[pltpu.VMEM((width, width), f32), pltpu.SemaphoreType.DMA((steps,))],
        compiler_params=pltpu.CompilerParams(vmem_limit_bytes=12 << 20),
        name="final",
    )(mine, other)


def swap(value, mask, count):
    return lax.ppermute(value, AXES, [(i, i ^ mask) for i in range(count)])


def combos(bits):
    masks = [0]
    for bit in bits:
        masks += [m | bit for m in masks]
    return masks


def gathered(tokens, norm_gains, enc_weight, head_weight, head_bias, positives):
    n_doc, count = lax.axis_size("doc"), lax.axis_size(AXES)
    seq, width = tokens.shape[1:]
    slots = positives.shape[1]
    core = n_doc
    bits = [1 << b for b in range(count.bit_length() - 1) if 1 << b != core]
    x, y, z, far = bits
    hop = functools.partial(swap, count=count)
    half, h = count // 2, seq // 2
    by_core = [i for i in range(count) if not i & core] + [i for i in range(count) if i & core]

    own = tokens.reshape(seq, width)
    held = {0: [(own, 0, seq)]}

    def exchange(plan, tied=()):
        come = {}
        for to, wanted in plan.items():
            parts = []
            for doc, low, high in wanted:
                at = 0
                for array, first, rows in held[doc]:
                    start, stop = max(low, at), min(high, at + rows)
                    if start < stop:
                        parts.append((array, first + start - at, stop - start))
                    at += rows
            come[to] = hop(parts[0][0] if not tied else join(parts, tied), to)
        new = {}
        for to, wanted in plan.items():
            at = 0
            for doc, low, high in wanted:
                new.setdefault(doc ^ to, []).append((low, come[to], at, high - low))
                at += high - low
        fresh = {}
        for doc, pieces in new.items():
            fresh[doc] = [piece[1:] for piece in sorted(pieces, key=lambda piece: piece[0])]
        held.update(fresh)
        return list(fresh), list(come.values())

    groups, masks = [], []

    def encode_held(docs):
        arrays, layout = [], []
        for doc in docs:
            pieces = []
            for array, first, rows in held[doc]:
                known = [k for k, a in enumerate(arrays) if a is array]
                if not known:
                    known = [len(arrays)]
                    arrays.append(array)
                pieces.append((known[0], first, rows))
            layout.append(pieces)
        groups.append(encode_call(arrays, layout, norm_gains, enc_weight))
        masks.append(docs)
        return groups[-1][2]

    whole = (0, 0, seq)
    docs_0, _ = exchange({far: [whole], z: [whole], x: [whole], y: [whole]})
    *group, copies = first_call(own, norm_gains, enc_weight, positives, count)
    groups.append(group)
    masks.append([0])
    rows = lax.all_to_all(copies, AXES, split_axis=0, concat_axis=0, tiled=True, axis_index_groups=[by_core])

    def spread(full, corners):
        wanted = [(doc, 0, seq) for doc in full]
        return {
            x: wanted + [(y | doc, 0, h) for doc in corners],
            y: wanted + [(x | doc, h, seq) for doc in corners],
        }

    early = mark([held[far][0][0]])
    plan = spread([z, far], [0])
    plan[z] = [(far, 0, seq)]
    docs_1, _ = exchange(plan, [groups[0][2], early])
    mine, other = pl.pallas_call(
        functools.partial(head_kernel, slots),
        out_shape=[jax.ShapeDtypeStruct((half, width), f32)] * 2,
        scratch_shapes=[pltpu.VMEM(rows.shape, f32), pltpu.VMEM((count, width), f32)],
        compiler_params=pltpu.CompilerParams(vmem_limit_bytes=10 << 20),
        name="head",
    )(rows, head_weight, head_bias)

    total = add([mine, hop(other, core)])
    plan = spread([z | far], [z, far])
    docs_2, _ = exchange(plan, [total])
    tied = encode_held(docs_0)
    total = add([total, hop(total, z)], [tied])
    tied = encode_held(docs_1[:4])
    total = add([total, hop(total, far)], [tied])
    plan = spread([], [z | far])
    docs_3, _ = exchange(plan, [total])
    rest = docs_1[4:]
    tied = [encode_held(rest)] if rest else []
    total = add([total, hop(total, x)], tied)
    tied = encode_held(docs_2)
    total = add([total, hop(total, y)], [tied])
    encode_held(docs_3)

    operands = [array for group in groups for array in group]
    part, row_grad = pl.pallas_call(
        functools.partial(back_kernel, seq, masks),
        out_shape=[
            jax.ShapeDtypeStruct((width + 16, width), bf16),
            jax.ShapeDtypeStruct((1, width), f32),
        ],
        scratch_shapes=[
            pltpu.VMEM((half * seq, width), bf16),
            pltpu.VMEM((half * seq, width), bf16),
            pltpu.VMEM((half, 8, width), f32),
            pltpu.VMEM((half, width), f32),
        ],
        compiler_params=pltpu.CompilerParams(vmem_limit_bytes=32 << 20),
        name="back",
    )(total, norm_gains, enc_weight, *operands)
    weight_grad, gain_grads = final_call(part, hop(part, core))
    return row_grad, weight_grad, gain_grads


def normalize(values):
    center = values - jnp.mean(values, axis=-1, keepdims=True)
    inverse = lax.rsqrt(jnp.mean(center * center, axis=-1, keepdims=True) + epsilon)
    return (center * inverse, inverse)


def encode(tok_block, gains, enc_weight):
    width = tok_block.shape[-1]
    tok_flat = tok_block.reshape(-1, width).astype(f32)
    normed_in, _ = normalize(tok_flat)
    act_in = (normed_in * gains[0]).astype(bf16)
    pre_act = jnp.dot(act_in, enc_weight, preferred_element_type=f32)
    hidden = tok_flat + jax.nn.gelu(pre_act)
    pooled = jnp.mean(hidden.reshape(tok_block.shape[0], tok_block.shape[1], width), axis=1)
    normed_out, inv_out = normalize(pooled)
    return (normed_out * gains[1], (normed_in, act_in, pre_act, normed_out, inv_out))


def encode_back(cotangent, saved, gains, enc_weight, seq_len):
    normed_in, act_in, pre_act, normed_out, inv_out = saved
    gain_out_grad = jnp.sum(cotangent * normed_out, axis=0)
    d_normed = cotangent * gains[1]
    d_pooled = inv_out * (
        d_normed
        - jnp.mean(d_normed, axis=-1, keepdims=True)
        - normed_out * jnp.mean(d_normed * normed_out, axis=-1, keepdims=True)
    )
    spread_grad = jnp.broadcast_to(
        (d_pooled / seq_len)[:, None, :], (d_pooled.shape[0], seq_len, d_pooled.shape[1])
    ).reshape(pre_act.shape)
    _, gelu_back = jax.vjp(jax.nn.gelu, pre_act)
    d_pre = gelu_back(spread_grad)[0]
    weight_grad = lax.dot_general(
        act_in.astype(f32), d_pre, (((0,), (0,)), ((), ())), precision=lax.Precision.HIGHEST, preferred_element_type=f32
    )
    d_act = lax.dot_general(
        d_pre, enc_weight.astype(f32), (((1,), (1,)), ((), ())), precision=lax.Precision.HIGHEST, preferred_element_type=f32
    )
    gain_in_grad = jnp.sum(d_act * normed_in, axis=0)
    return (weight_grad, jnp.stack([gain_in_grad, gain_out_grad]))


def head_block(embed_bf, label_lists, weight_block, bias_block, first_label):
    logits = lax.dot_general(embed_bf, weight_block, (((1,), (1,)), ((), ())), preferred_element_type=f32)
    logits = logits + bias_block.astype(f32)[None, :]
    label_ids = first_label + jnp.arange(weight_block.shape[0], dtype=jnp.int32)
    target = jnp.any(label_lists[:, :, None] == label_ids[None, None, :], axis=1).astype(f32)
    d_logit = (jax.nn.sigmoid(logits) - target).astype(bf16)
    return jnp.dot(d_logit, weight_block, preferred_element_type=f32)


def spread_out(tokens, norm_gains, enc_weight, head_weight, head_bias, positives):
    doc_count, seq_len, width = tokens.shape
    embed, saved = encode(tokens, norm_gains, enc_weight)
    col_embed, col_lists = (
        lax.all_gather(embed.astype(bf16), "label", axis=0, tiled=True),
        lax.all_gather(positives, "label", axis=0, tiled=True),
    )
    span = head_weight.shape[0] * lax.axis_size("doc")
    partial_grad = head_block(
        col_embed,
        col_lists,
        lax.all_gather(head_weight, "doc", axis=0, tiled=True),
        lax.all_gather(head_bias, "doc", axis=0, tiled=True),
        lax.axis_index("label") * span,
    )
    summed = lax.psum(partial_grad, "label")
    row_grad = lax.dynamic_slice_in_dim(summed, lax.axis_index("label") * doc_count, doc_count, 0)
    weight_part, gain_part = encode_back(row_grad, saved, norm_gains, enc_weight, seq_len)
    weight_grad, gain_grads = lax.psum((weight_part, gain_part), AXES)
    return (row_grad, weight_grad, gain_grads)


def shards(tokens, *rest):
    count = lax.axis_size(AXES)
    powers = all(size & (size - 1) == 0 for size in (count, lax.axis_size("doc")))
    fits = tokens.size * tokens.dtype.itemsize * (count // 2) <= GATHER_LIMIT
    plan = gathered if fits and powers and count == 32 and tokens.shape[0] == 1 else spread_out
    return plan(tokens, *rest)


def solution(mesh):
    placed = (
        P(AXES, None, None),
        P(),
        P(),
        P(AXES, None),
        P(AXES),
        P(AXES, None),
    )
    return jax.shard_map(
        shards,
        mesh=mesh,
        in_specs=placed,
        out_specs=(P(AXES, None), P(), P()),
        check_vma=False,
    )
```

```python
import functools
import math

import jax
import jax.numpy as jnp
from jax import lax
from jax.experimental import pallas as pl
from jax.experimental.pallas import tpu as pltpu
from jax.sharding import PartitionSpec as P

epsilon = 1e-05
AXES = ("label", "doc")
PIECE_BITS = 8
PIECE = 1 << PIECE_BITS
DIGITS = 3
GATHER_LIMIT = 8 << 20
FIRST_LIMIT = 10 << 20
f32, bf16 = jnp.float32, jnp.bfloat16


def enter(tok, gains):
    values = tok.astype(f32)
    center = values - jnp.mean(values, axis=-1, keepdims=True)
    inverse = lax.rsqrt(jnp.mean(center * center, axis=-1, keepdims=True) + epsilon)
    act = (center * inverse * gains[0:1]).astype(bf16)
    return act, jnp.sum(act.astype(f32), axis=0, keepdims=True)


def bend(tok, pre):
    scale = math.sqrt(2.0 / math.pi)
    square = pre * pre
    half = 0.5 * jnp.tanh(pre * (scale + (scale * 0.044715) * square))
    gelu = pre * (0.5 + half)
    tilt = half + gelu * (0.5 - half) * (2.0 * scale + (6.0 * scale * 0.044715) * square)
    return tilt, jnp.sum(tok.astype(f32) + gelu, axis=0, keepdims=True)


def norm_row(pooled):
    center = pooled - jnp.mean(pooled, axis=-1, keepdims=True)
    inverse = lax.rsqrt(jnp.mean(center * center, axis=-1, keepdims=True) + epsilon)
    return center * inverse, inverse


def place(device, core):
    return (device // (2 * core)) * core + device % core


def number():
    return lax.axis_index("label") * lax.axis_size("doc") + lax.axis_index("doc")


def encode_into(layout, toks, gains, weight, act_ref, tilt_ref, row_ref):
    seq = sum(rows for _, _, rows in layout[0])
    span = seq // 2
    halves = []
    for doc in layout:
        for operand, first, rows in doc:
            halves += [(operand, first + start) for start in range(0, rows, span)]
    acts = []
    for k, (operand, first) in enumerate(halves):
        act, sums = enter(toks[operand][first : first + span, :], gains)
        act_ref[k * span : (k + 1) * span, :] = act
        acts.append(sums)
    totals = []
    for k, (operand, first) in enumerate(halves):
        if k % 2 == 0:
            pre = jnp.dot(act_ref[k * span : (k + 2) * span, :], weight, preferred_element_type=f32)
        tilt, sums = bend(toks[operand][first : first + span, :], pre[k % 2 * span : (k % 2 + 1) * span])
        tilt_ref[k * span : (k + 1) * span, :] = tilt
        totals.append(sums)
    for d in range(len(layout)):
        normed, inverse = norm_row((totals[2 * d] + totals[2 * d + 1]) * (1.0 / seq))
        row_ref[d, 0:1, :] = normed
        row_ref[d, 1:2, :] = jnp.broadcast_to(inverse, normed.shape)
        row_ref[d, 2:3, :] = acts[2 * d] + acts[2 * d + 1]
    return normed


def first_kernel(*refs):
    sources, (act_ref, tilt_ref, row_ref, embed_ref), held, (digits, sems) = refs[:4], refs[4:8], refs[8:12], refs[12:]
    copies = [pltpu.make_async_copy(a, b, sems.at[k]) for k, (a, b) in enumerate(zip(sources, held, strict=True))]
    for copy in copies:
        copy.start()
    for copy in copies:
        copy.wait()
    tok, gains_ref, weight_ref, listed_ref = held
    gains = gains_ref[...]
    seq, width = tok.shape
    slots = listed_ref.shape[1]
    normed = encode_into([[(0, 0, seq)]], [tok], gains, weight_ref[...], act_ref, tilt_ref, row_ref)
    embed = normed * gains[1:2]
    digits[...] = jnp.zeros_like(digits)
    shifted = listed_ref[...] + 1
    for k in range(DIGITS):
        digit = jnp.bitwise_and(jnp.right_shift(shifted, PIECE_BITS * (DIGITS - 1 - k)), PIECE - 1)
        digits[:, k * slots : (k + 1) * slots] = digit.astype(f32)
    lanes = [embed[:, k * 128 : (k + 1) * 128] for k in range(width // 128)] + [digits[...]]
    lanes += [jnp.zeros((1, 128), f32)] * (embed_ref.shape[1] - len(lanes))
    block = jnp.concatenate(lanes, axis=0).astype(bf16)
    embed_ref[...] = jnp.broadcast_to(block[None], embed_ref.shape)


def encode_kernel(layout, *refs):
    toks, (gains_ref, weight_ref, act_ref, tilt_ref, row_ref) = refs[:-5], refs[-5:]
    encode_into(layout, toks, gains_ref[...], weight_ref[...], act_ref, tilt_ref, row_ref)


def encode_shapes(rows, docs, width):
    return [
        jax.ShapeDtypeStruct((rows, width), bf16),
        jax.ShapeDtypeStruct((rows, width), f32),
        jax.ShapeDtypeStruct((docs, 8, width), f32),
    ]


def first_call(own, gains, weight, listed, copies):
    seq, width = own.shape
    sources = [own, gains, weight, listed]
    deep = -(-(width // 128 + 1) // 8) * 8
    return pl.pallas_call(
        first_kernel,
        out_shape=encode_shapes(seq, 1, width) + [jax.ShapeDtypeStruct((copies, deep, 128), bf16)],
        in_specs=[pl.BlockSpec(memory_space=pltpu.HBM)] * 4,
        scratch_shapes=[pltpu.VMEM(a.shape, a.dtype) for a in sources]
        + [pltpu.VMEM((1, 128), f32), pltpu.SemaphoreType.DMA((4,))],
        compiler_params=pltpu.CompilerParams(vmem_limit_bytes=FIRST_LIMIT),
        name="first",
    )(*sources)


def encode_call(arrays, layout, gains, weight):
    rows = sum(piece[2] for doc in layout for piece in doc)
    return pl.pallas_call(
        functools.partial(encode_kernel, layout),
        out_shape=encode_shapes(rows, len(layout), gains.shape[1]),
        compiler_params=pltpu.CompilerParams(vmem_limit_bytes=14 << 20),
        name="encode",
    )(*arrays, gains, weight)


def join_kernel(pieces, *refs):
    out_ref = refs[-1]
    at = 0
    for operand, first, rows in pieces:
        out_ref[at : at + rows, :] = refs[operand][first : first + rows, :]
        at += rows


def join(parts, tied=()):
    arrays, pieces = [], []
    for array, first, rows in parts:
        known = [k for k, a in enumerate(arrays) if a is array]
        if not known:
            known = [len(arrays)]
            arrays.append(array)
        pieces.append((known[0], first, rows))
    vmem, anywhere = pl.BlockSpec(memory_space=pltpu.VMEM), pl.BlockSpec(memory_space=pl.ANY)
    return pl.pallas_call(
        functools.partial(join_kernel, pieces),
        out_shape=jax.ShapeDtypeStruct((sum(p[2] for p in pieces), arrays[0].shape[1]), arrays[0].dtype),
        in_specs=[vmem] * len(arrays) + [anywhere] * len(tied),
        compiler_params=pltpu.CompilerParams(vmem_limit_bytes=4 << 20),
        name="join",
    )(*arrays, *tied)


def add_kernel(count, *refs):
    parts = [ref[...] for ref in refs[:count]]
    while len(parts) > 1:
        parts = [parts[i] + parts[i + 1] for i in range(0, len(parts), 2)]
    refs[-1][...] = parts[0]


def add(parts, tied=()):
    vmem, anywhere = pl.BlockSpec(memory_space=pltpu.VMEM), pl.BlockSpec(memory_space=pl.ANY)
    return pl.pallas_call(
        functools.partial(add_kernel, len(parts)),
        out_shape=jax.ShapeDtypeStruct(parts[0].shape, parts[0].dtype),
        in_specs=[vmem] * len(parts) + [anywhere] * len(tied),
        compiler_params=pltpu.CompilerParams(vmem_limit_bytes=4 << 20),
        name="add",
    )(*parts, *tied)


def mark_kernel(*refs):
    refs[-1][...] = jnp.zeros_like(refs[-1])


def mark(arrays):
    return pl.pallas_call(
        mark_kernel,
        out_shape=jax.ShapeDtypeStruct((8, 128), f32),
        in_specs=[pl.BlockSpec(memory_space=pl.ANY)] * len(arrays),
        compiler_params=pltpu.CompilerParams(vmem_limit_bytes=1 << 20),
        name="mark",
    )(*arrays)


def head_kernel(slots, rows_ref, weight_ref, bias_ref, mine_ref, other_ref, rows, part):
    labels, width = weight_ref.shape
    lanes = width // 128 + 1
    me, core = number(), lax.axis_size("doc")
    rows[...] = rows_ref[...].astype(f32)
    weight = weight_ref[...]
    embed = jnp.concatenate([rows[:, k, :] for k in range(lanes - 1)], axis=1)
    logits = lax.dot_general(
        embed.astype(bf16), weight, (((1,), (1,)), ((), ())), preferred_element_type=f32
    ) + bias_ref[...].astype(f32).reshape(1, labels)
    digits = rows[:, lanes - 1, :]
    ids = digits[:, :slots] * (PIECE * PIECE) + digits[:, slots : 2 * slots] * PIECE + digits[:, 2 * slots : 3 * slots]
    own = lax.broadcasted_iota(jnp.int32, logits.shape, 1) + (me * labels + 1)
    listed = ids.astype(jnp.int32)
    hit = own == listed[:, 0:1]
    for k in range(1, slots):
        hit = jnp.logical_or(hit, own == listed[:, k : k + 1])
    d_logit = (jax.nn.sigmoid(logits) - jnp.where(hit, 1.0, 0.0)).astype(bf16)
    part[...] = jnp.dot(d_logit, weight, preferred_element_type=f32)
    half = part.shape[0] // 2
    kind = lax.rem(me // core, 2)
    mine_ref[...] = part[pl.ds(pl.multiple_of(kind * half, half), half), :]
    other_ref[...] = part[pl.ds(pl.multiple_of((1 - kind) * half, half), half), :]


def share(first, acts, d_pre, factors, gains, weight_ref, out_ref, act):
    half, width = act.shape[1], d_pre.shape[1]
    columns = pl.ds(first, half)
    base = 0
    for ref in acts:
        act[pl.ds(base, ref.shape[0]), :] = ref[:, columns]
        base += ref.shape[0]
    left, right = factors
    even = lax.dot_general(left[:, columns], right[...], (((0,), (0,)), ((), ())), preferred_element_type=f32)
    total = even + lax.dot_general(act[...], d_pre[...], (((0,), (0,)), ((), ())), preferred_element_type=f32)
    out_ref[:half, :] = total.astype(bf16)
    weighed = total * weight_ref[columns, :].astype(f32)
    lanes = weighed[:, :128]
    for k in range(1, width // 128):
        lanes = lanes + weighed[:, k * 128 : (k + 1) * 128]
    gain_in = jnp.sum(lanes.T, axis=0, keepdims=True) / gains[:, columns]
    none = jnp.zeros((1, width - half), f32)
    return jnp.concatenate([none, gain_in] if first else [gain_in, none], axis=1)


def terms(values):
    parts = []
    for rest in values:
        for _ in range(3):
            parts.append(rest.astype(bf16).astype(f32))
            rest = rest - parts[-1]
    return jnp.concatenate(parts + [jnp.zeros((16 - len(parts), rest.shape[1]), f32)], axis=0).astype(bf16)


def back_kernel(seq, masks, *refs):
    grad_ref, gains_ref, weight_ref = refs[:3]
    groups = [refs[3 + 3 * g : 6 + 3 * g] for g in range(len(masks))]
    out_ref, own_ref, d_pre, left, right, act, saved, spreads, own, sem = refs[3 + 3 * len(masks) :]
    me, core = number(), lax.axis_size("doc")
    places = [[place(me ^ m, core) for m in group] for group in masks]
    own[...] = grad_ref[pl.ds(place(me, core), 1), :]
    copy = pltpu.make_async_copy(own, own_ref, sem)
    copy.start()
    half = weight_ref.shape[0] // 2
    for (_, _, row_ref), group in zip(groups, places, strict=True):
        for d, at in enumerate(group):
            saved[at] = row_ref[d]
    row, normed, inverse, sums = grad_ref[...], saved[:, 0, :], saved[:, 1, :], saved[:, 2, :]
    d_normed = row * gains_ref[1:2, :]
    spread = (
        inverse
        * (
            d_normed
            - jnp.mean(d_normed, axis=-1, keepdims=True)
            - normed * jnp.mean(d_normed * normed, axis=-1, keepdims=True)
        )
        * (1.0 / seq)
    )
    spreads[...] = spread
    even = 0.5 * spread
    sums_top, even_top = sums.astype(bf16), even.astype(bf16)
    sums_low = (sums - sums_top.astype(f32)).astype(bf16)
    even_low = (even - even_top.astype(f32)).astype(bf16)
    left[...] = jnp.concatenate([sums_top, sums_top, sums_low], axis=0)
    right[...] = jnp.concatenate([even_top, even_low, even_top], axis=0)
    base = 0
    for (_, tilt_ref, _), group in zip(groups, places, strict=True):
        for d, at in enumerate(group):
            d_pre[pl.ds(base, seq), :] = (tilt_ref[d * seq : (d + 1) * seq, :] * spreads[pl.ds(at, 1), :]).astype(bf16)
            base += seq
    acts = [act_ref for act_ref, _, _ in groups]
    gain_in = share(0, acts, d_pre, (left, right), gains_ref[0:1, :], weight_ref, out_ref, act)
    out_ref[half:, :] = terms([jnp.sum(row * normed, axis=0, keepdims=True), gain_in])
    copy.wait()


def more_kernel(*refs):
    (gains_ref, weight_ref, d_pre, left, right), acts, (out_ref, act) = refs[:5], refs[5:-2], refs[-2:]
    half = weight_ref.shape[0] // 2
    gain_in = share(half, acts, d_pre, (left, right), gains_ref[0:1, :], weight_ref, out_ref, act)
    out_ref[half:, :] = terms([jnp.zeros_like(gain_in), gain_in])


def back_calls(seq, masks, total, gains, weight, groups):
    width, docs = weight.shape[0], sum(len(group) for group in masks)
    half = width // 2
    share_shape = jax.ShapeDtypeStruct((half + 16, width), bf16)
    act, vmem = pltpu.VMEM((docs * seq, half), bf16), pl.BlockSpec(memory_space=pltpu.VMEM)
    top, row_grad, *middle = pl.pallas_call(
        functools.partial(back_kernel, seq, masks),
        out_shape=[
            share_shape,
            jax.ShapeDtypeStruct((1, width), f32),
            jax.ShapeDtypeStruct((docs * seq, width), bf16),
            jax.ShapeDtypeStruct((3 * docs, width), bf16),
            jax.ShapeDtypeStruct((3 * docs, width), bf16),
        ],
        out_specs=[vmem, pl.BlockSpec(memory_space=pltpu.HBM), vmem, vmem, vmem],
        scratch_shapes=[
            act,
            pltpu.VMEM((docs, 8, width), f32),
            pltpu.VMEM((docs, width), f32),
            pltpu.VMEM((1, width), f32),
            pltpu.SemaphoreType.DMA,
        ],
        compiler_params=pltpu.CompilerParams(vmem_limit_bytes=32 << 20),
        name="back",
    )(total, gains, weight, *[array for group in groups for array in group])
    low = pl.pallas_call(
        more_kernel,
        out_shape=share_shape,
        scratch_shapes=[act],
        compiler_params=pltpu.CompilerParams(vmem_limit_bytes=24 << 20),
        name="more",
    )(gains, weight, *middle, *[group[0] for group in groups])
    return top, low, row_grad


def final_kernel(first, *refs):
    (mine_ref, other_ref), weight_ref, (total, gains, sems) = refs[:2], refs[-4 - (first > 0)], refs[-3:]
    rows, steps = total.shape[0], sems.shape[0] - 1
    span = rows // steps
    copies = []
    if first:
        gain_in = gain_out = 0.0
        for pair in (refs[:2], refs[2:4]):
            mine, other = pair[0][rows:, :].astype(f32), pair[1][rows:, :].astype(f32)
            gain_out += (mine[0:1] + mine[1:2] + mine[2:3]) + (other[0:1] + other[1:2] + other[2:3])
            gain_in += (mine[3:4] + mine[4:5] + mine[5:6]) + (other[3:4] + other[4:5] + other[5:6])
        gains[...] = jnp.concatenate([gain_in, gain_out], axis=0)
        copies.append(pltpu.make_async_copy(gains, refs[-4], sems.at[steps]))
        copies[-1].start()
    for k in range(steps):
        part = pl.ds(k * span, span)
        total[part, :] = mine_ref[part, :].astype(f32) + other_ref[part, :].astype(f32)
        copies.append(pltpu.make_async_copy(total.at[part, :], weight_ref.at[pl.ds(first + k * span, span), :], sems.at[k]))
        copies[-1].start()
    for copy in copies:
        copy.wait()


def final_call(first, shares, before=None):
    rows, width = shares[0].shape[0] - 16, shares[0].shape[1]
    steps = 4 if rows % 64 == 0 else 1
    vmem, hbm = pl.BlockSpec(memory_space=pltpu.VMEM), pl.BlockSpec(memory_space=pltpu.HBM)
    extra = [] if before is None else [before]
    return pl.pallas_call(
        functools.partial(final_kernel, first),
        out_shape=[jax.ShapeDtypeStruct((2 * rows, width), f32)] + [jax.ShapeDtypeStruct((2, width), f32)] * len(extra),
        in_specs=[vmem] * len(shares) + [hbm] * len(extra),
        out_specs=[hbm] * (1 + len(extra)),
        input_output_aliases={len(shares): 0} if extra else {},
        scratch_shapes=[
            pltpu.VMEM((rows, width), f32),
            pltpu.VMEM((2, width), f32),
            pltpu.SemaphoreType.DMA((steps + 1,)),
        ],
        compiler_params=pltpu.CompilerParams(vmem_limit_bytes=12 << 20),
        name="final",
    )(*shares, *extra)


def swap(value, mask, count):
    return lax.ppermute(value, AXES, [(i, i ^ mask) for i in range(count)])


def combos(bits):
    masks = [0]
    for bit in bits:
        masks += [m | bit for m in masks]
    return masks


def gathered(tokens, norm_gains, enc_weight, head_weight, head_bias, positives):
    n_doc, count = lax.axis_size("doc"), lax.axis_size(AXES)
    seq, width = tokens.shape[1:]
    slots = positives.shape[1]
    core = n_doc
    bits = [1 << b for b in range(count.bit_length() - 1) if 1 << b != core]
    x, y, z, far = bits
    hop = functools.partial(swap, count=count)
    half, h = count // 2, seq // 2
    by_core = [i for i in range(count) if not i & core] + [i for i in range(count) if i & core]

    own = tokens.reshape(seq, width)
    held = {0: [(own, 0, seq)]}

    def exchange(plan, tied=()):
        come = {}
        for to, wanted in plan.items():
            parts = []
            for doc, low, high in wanted:
                at = 0
                for array, first, rows in held[doc]:
                    start, stop = max(low, at), min(high, at + rows)
                    if start < stop:
                        parts.append((array, first + start - at, stop - start))
                    at += rows
            come[to] = hop(parts[0][0] if not tied else join(parts, tied), to)
        new = {}
        for to, wanted in plan.items():
            at = 0
            for doc, low, high in wanted:
                new.setdefault(doc ^ to, []).append((low, come[to], at, high - low))
                at += high - low
        fresh = {}
        for doc, pieces in new.items():
            fresh[doc] = [piece[1:] for piece in sorted(pieces, key=lambda piece: piece[0])]
        held.update(fresh)
        return list(fresh), list(come.values())

    groups, masks = [], []

    def encode_held(docs):
        arrays, layout = [], []
        for doc in docs:
            pieces = []
            for array, first, rows in held[doc]:
                known = [k for k, a in enumerate(arrays) if a is array]
                if not known:
                    known = [len(arrays)]
                    arrays.append(array)
                pieces.append((known[0], first, rows))
            layout.append(pieces)
        groups.append(encode_call(arrays, layout, norm_gains, enc_weight))
        masks.append(docs)
        return groups[-1][2]

    whole = (0, 0, seq)
    docs_0, _ = exchange({far: [whole], z: [whole], x: [whole], y: [whole]})
    *group, copies = first_call(own, norm_gains, enc_weight, positives, count)
    groups.append(group)
    masks.append([0])
    rows = lax.all_to_all(copies, AXES, split_axis=0, concat_axis=0, tiled=True, axis_index_groups=[by_core])

    def spread(full, corners):
        wanted = [(doc, 0, seq) for doc in full]
        return {
            x: wanted + [(y | doc, 0, h) for doc in corners],
            y: wanted + [(x | doc, h, seq) for doc in corners],
        }

    early = mark([held[far][0][0]])
    plan = spread([z, far], [0])
    plan[z] = [(far, 0, seq)]
    docs_1, _ = exchange(plan, [groups[0][2], early])
    mine, other = pl.pallas_call(
        functools.partial(head_kernel, slots),
        out_shape=[jax.ShapeDtypeStruct((half, width), f32)] * 2,
        scratch_shapes=[pltpu.VMEM(rows.shape, f32), pltpu.VMEM((count, width), f32)],
        compiler_params=pltpu.CompilerParams(vmem_limit_bytes=10 << 20),
        name="head",
    )(rows, head_weight, head_bias)

    total = add([mine, hop(other, core)])
    plan = spread([z | far], [z, far])
    docs_2, _ = exchange(plan, [total])
    tied = encode_held(docs_0)
    total = add([total, hop(total, z)], [tied])
    tied = encode_held(docs_1[:4])
    total = add([total, hop(total, far)], [tied])
    plan = spread([], [z | far])
    docs_3, _ = exchange(plan, [total])
    rest = docs_1[4:]
    tied = [encode_held(rest)] if rest else []
    total = add([total, hop(total, x)], tied)
    tied = [encode_held(docs_2), encode_held(docs_3)]
    total = add([total, hop(total, y)], tied)

    top, low, row_grad = back_calls(seq, masks, total, norm_gains, enc_weight, groups)
    other_top, other_low = hop(top, core), hop(low, core)
    (weight_grad,) = final_call(0, [top, other_top])
    weight_grad, gain_grads = final_call(width // 2, [low, other_low, top, other_top], weight_grad)
    return row_grad, weight_grad, gain_grads


def normalize(values):
    center = values - jnp.mean(values, axis=-1, keepdims=True)
    inverse = lax.rsqrt(jnp.mean(center * center, axis=-1, keepdims=True) + epsilon)
    return (center * inverse, inverse)


def encode(tok_block, gains, enc_weight):
    width = tok_block.shape[-1]
    tok_flat = tok_block.reshape(-1, width).astype(f32)
    normed_in, _ = normalize(tok_flat)
    act_in = (normed_in * gains[0]).astype(bf16)
    pre_act = jnp.dot(act_in, enc_weight, preferred_element_type=f32)
    hidden = tok_flat + jax.nn.gelu(pre_act)
    pooled = jnp.mean(hidden.reshape(tok_block.shape[0], tok_block.shape[1], width), axis=1)
    normed_out, inv_out = normalize(pooled)
    return (normed_out * gains[1], (normed_in, act_in, pre_act, normed_out, inv_out))


def encode_back(cotangent, saved, gains, enc_weight, seq_len):
    normed_in, act_in, pre_act, normed_out, inv_out = saved
    gain_out_grad = jnp.sum(cotangent * normed_out, axis=0)
    d_normed = cotangent * gains[1]
    d_pooled = inv_out * (
        d_normed
        - jnp.mean(d_normed, axis=-1, keepdims=True)
        - normed_out * jnp.mean(d_normed * normed_out, axis=-1, keepdims=True)
    )
    spread_grad = jnp.broadcast_to(
        (d_pooled / seq_len)[:, None, :], (d_pooled.shape[0], seq_len, d_pooled.shape[1])
    ).reshape(pre_act.shape)
    _, gelu_back = jax.vjp(jax.nn.gelu, pre_act)
    d_pre = gelu_back(spread_grad)[0]
    weight_grad = lax.dot_general(
        act_in.astype(f32), d_pre, (((0,), (0,)), ((), ())), precision=lax.Precision.HIGHEST, preferred_element_type=f32
    )
    d_act = lax.dot_general(
        d_pre, enc_weight.astype(f32), (((1,), (1,)), ((), ())), precision=lax.Precision.HIGHEST, preferred_element_type=f32
    )
    gain_in_grad = jnp.sum(d_act * normed_in, axis=0)
    return (weight_grad, jnp.stack([gain_in_grad, gain_out_grad]))


def head_block(embed_bf, label_lists, weight_block, bias_block, first_label):
    logits = lax.dot_general(embed_bf, weight_block, (((1,), (1,)), ((), ())), preferred_element_type=f32)
    logits = logits + bias_block.astype(f32)[None, :]
    label_ids = first_label + jnp.arange(weight_block.shape[0], dtype=jnp.int32)
    target = jnp.any(label_lists[:, :, None] == label_ids[None, None, :], axis=1).astype(f32)
    d_logit = (jax.nn.sigmoid(logits) - target).astype(bf16)
    return jnp.dot(d_logit, weight_block, preferred_element_type=f32)


def spread_out(tokens, norm_gains, enc_weight, head_weight, head_bias, positives):
    doc_count, seq_len, width = tokens.shape
    embed, saved = encode(tokens, norm_gains, enc_weight)
    col_embed, col_lists = (
        lax.all_gather(embed.astype(bf16), "label", axis=0, tiled=True),
        lax.all_gather(positives, "label", axis=0, tiled=True),
    )
    span = head_weight.shape[0] * lax.axis_size("doc")
    partial_grad = head_block(
        col_embed,
        col_lists,
        lax.all_gather(head_weight, "doc", axis=0, tiled=True),
        lax.all_gather(head_bias, "doc", axis=0, tiled=True),
        lax.axis_index("label") * span,
    )
    summed = lax.psum(partial_grad, "label")
    row_grad = lax.dynamic_slice_in_dim(summed, lax.axis_index("label") * doc_count, doc_count, 0)
    weight_part, gain_part = encode_back(row_grad, saved, norm_gains, enc_weight, seq_len)
    weight_grad, gain_grads = lax.psum((weight_part, gain_part), AXES)
    return (row_grad, weight_grad, gain_grads)


def shards(tokens, *rest):
    count = lax.axis_size(AXES)
    powers = all(size & (size - 1) == 0 for size in (count, lax.axis_size("doc")))
    fits = tokens.size * tokens.dtype.itemsize * (count // 2) <= GATHER_LIMIT
    plan = gathered if fits and powers and count == 32 and tokens.shape[0] == 1 else spread_out
    return plan(tokens, *rest)


def solution(mesh):
    placed = (
        P(AXES, None, None),
        P(),
        P(),
        P(AXES, None),
        P(AXES),
        P(AXES, None),
    )
    return jax.shard_map(
        shards,
        mesh=mesh,
        in_specs=placed,
        out_specs=(P(AXES, None), P(), P()),
        check_vma=False,
    )
```

```python
import functools
import math

import jax
import jax.numpy as jnp
from jax import lax
from jax.experimental import pallas as pl
from jax.experimental.pallas import tpu as pltpu
from jax.sharding import PartitionSpec as P

epsilon = 1e-05
AXES = ("label", "doc")
PIECE_BITS = 8
PIECE = 1 << PIECE_BITS
DIGITS = 3
GATHER_LIMIT = 8 << 20
FIRST_LIMIT = 10 << 20
f32, bf16 = jnp.float32, jnp.bfloat16


def enter(tok, gains):
    values = tok.astype(f32)
    center = values - jnp.mean(values, axis=-1, keepdims=True)
    inverse = lax.rsqrt(jnp.mean(center * center, axis=-1, keepdims=True) + epsilon)
    act = (center * inverse * gains[0:1]).astype(bf16)
    return act, jnp.sum(act.astype(f32), axis=0, keepdims=True)


def bend(tok, pre):
    scale = math.sqrt(2.0 / math.pi)
    square = pre * pre
    half = 0.5 * jnp.tanh(pre * (scale + (scale * 0.044715) * square))
    gelu = pre * (0.5 + half)
    tilt = half + gelu * (0.5 - half) * (2.0 * scale + (6.0 * scale * 0.044715) * square)
    return tilt, jnp.sum(tok.astype(f32) + gelu, axis=0, keepdims=True)


def norm_row(pooled):
    center = pooled - jnp.mean(pooled, axis=-1, keepdims=True)
    inverse = lax.rsqrt(jnp.mean(center * center, axis=-1, keepdims=True) + epsilon)
    return center * inverse, inverse


def place(device, core):
    return (device // (2 * core)) * core + device % core


def number():
    return lax.axis_index("label") * lax.axis_size("doc") + lax.axis_index("doc")


def encode_into(layout, toks, gains, weight, act_ref, tilt_ref, row_ref):
    seq = sum(rows for _, _, rows in layout[0])
    span = seq // 2
    halves = []
    for doc in layout:
        for operand, first, rows in doc:
            halves += [(operand, first + start) for start in range(0, rows, span)]
    acts = []
    for k, (operand, first) in enumerate(halves):
        act, sums = enter(toks[operand][first : first + span, :], gains)
        act_ref[k * span : (k + 1) * span, :] = act
        acts.append(sums)
    totals = []
    for k, (operand, first) in enumerate(halves):
        if k % 2 == 0:
            pre = jnp.dot(act_ref[k * span : (k + 2) * span, :], weight, preferred_element_type=f32)
        tilt, sums = bend(toks[operand][first : first + span, :], pre[k % 2 * span : (k % 2 + 1) * span])
        tilt_ref[k * span : (k + 1) * span, :] = tilt
        totals.append(sums)
    for d in range(len(layout)):
        normed, inverse = norm_row((totals[2 * d] + totals[2 * d + 1]) * (1.0 / seq))
        row_ref[d, 0:1, :] = normed
        row_ref[d, 1:2, :] = jnp.broadcast_to(inverse, normed.shape)
        row_ref[d, 2:3, :] = acts[2 * d] + acts[2 * d + 1]
    return normed


def first_kernel(*refs):
    sources, (act_ref, tilt_ref, row_ref, embed_ref), held, (digits, sems) = refs[:4], refs[4:8], refs[8:12], refs[12:]
    copies = [pltpu.make_async_copy(a, b, sems.at[k]) for k, (a, b) in enumerate(zip(sources, held, strict=True))]
    for copy in copies:
        copy.start()
    for copy in copies:
        copy.wait()
    tok, gains_ref, weight_ref, listed_ref = held
    gains = gains_ref[...]
    seq, width = tok.shape
    slots = listed_ref.shape[1]
    normed = encode_into([[(0, 0, seq)]], [tok], gains, weight_ref[...], act_ref, tilt_ref, row_ref)
    embed = normed * gains[1:2]
    digits[...] = jnp.zeros_like(digits)
    shifted = listed_ref[...] + 1
    for k in range(DIGITS):
        digit = jnp.bitwise_and(jnp.right_shift(shifted, PIECE_BITS * (DIGITS - 1 - k)), PIECE - 1)
        digits[:, k * slots : (k + 1) * slots] = digit.astype(f32)
    lanes = [embed[:, k * 128 : (k + 1) * 128] for k in range(width // 128)] + [digits[...]]
    lanes += [jnp.zeros((1, 128), f32)] * (embed_ref.shape[1] - len(lanes))
    block = jnp.concatenate(lanes, axis=0).astype(bf16)
    embed_ref[...] = jnp.broadcast_to(block[None], embed_ref.shape)


def encode_kernel(layout, *refs):
    toks, (gains_ref, weight_ref, act_ref, tilt_ref, row_ref) = refs[:-5], refs[-5:]
    encode_into(layout, toks, gains_ref[...], weight_ref[...], act_ref, tilt_ref, row_ref)


def encode_shapes(rows, docs, width):
    return [
        jax.ShapeDtypeStruct((rows, width), bf16),
        jax.ShapeDtypeStruct((rows, width), f32),
        jax.ShapeDtypeStruct((docs, 8, width), f32),
    ]


def first_call(own, gains, weight, listed, copies):
    seq, width = own.shape
    sources = [own, gains, weight, listed]
    deep = -(-(width // 128 + 1) // 8) * 8
    return pl.pallas_call(
        first_kernel,
        out_shape=encode_shapes(seq, 1, width) + [jax.ShapeDtypeStruct((copies, deep, 128), bf16)],
        in_specs=[pl.BlockSpec(memory_space=pltpu.HBM)] * 4,
        scratch_shapes=[pltpu.VMEM(a.shape, a.dtype) for a in sources]
        + [pltpu.VMEM((1, 128), f32), pltpu.SemaphoreType.DMA((4,))],
        compiler_params=pltpu.CompilerParams(vmem_limit_bytes=FIRST_LIMIT),
        name="first",
    )(*sources)


def encode_call(arrays, layout, gains, weight):
    rows = sum(piece[2] for doc in layout for piece in doc)
    return pl.pallas_call(
        functools.partial(encode_kernel, layout),
        out_shape=encode_shapes(rows, len(layout), gains.shape[1]),
        compiler_params=pltpu.CompilerParams(vmem_limit_bytes=14 << 20),
        name="encode",
    )(*arrays, gains, weight)


def join_kernel(pieces, *refs):
    out_ref = refs[-1]
    at = 0
    for operand, first, rows in pieces:
        out_ref[at : at + rows, :] = refs[operand][first : first + rows, :]
        at += rows


def join(parts, tied=()):
    arrays, pieces = [], []
    for array, first, rows in parts:
        known = [k for k, a in enumerate(arrays) if a is array]
        if not known:
            known = [len(arrays)]
            arrays.append(array)
        pieces.append((known[0], first, rows))
    vmem, anywhere = pl.BlockSpec(memory_space=pltpu.VMEM), pl.BlockSpec(memory_space=pl.ANY)
    return pl.pallas_call(
        functools.partial(join_kernel, pieces),
        out_shape=jax.ShapeDtypeStruct((sum(p[2] for p in pieces), arrays[0].shape[1]), arrays[0].dtype),
        in_specs=[vmem] * len(arrays) + [anywhere] * len(tied),
        compiler_params=pltpu.CompilerParams(vmem_limit_bytes=4 << 20),
        name="join",
    )(*arrays, *tied)


def add_kernel(count, *refs):
    parts = [ref[...] for ref in refs[:count]]
    while len(parts) > 1:
        parts = [parts[i] + parts[i + 1] for i in range(0, len(parts), 2)]
    refs[-1][...] = parts[0]


def add(parts, tied=()):
    vmem, anywhere = pl.BlockSpec(memory_space=pltpu.VMEM), pl.BlockSpec(memory_space=pl.ANY)
    return pl.pallas_call(
        functools.partial(add_kernel, len(parts)),
        out_shape=jax.ShapeDtypeStruct(parts[0].shape, parts[0].dtype),
        in_specs=[vmem] * len(parts) + [anywhere] * len(tied),
        compiler_params=pltpu.CompilerParams(vmem_limit_bytes=4 << 20),
        name="add",
    )(*parts, *tied)


def mark_kernel(*refs):
    refs[-1][...] = jnp.zeros_like(refs[-1])


def mark(arrays):
    return pl.pallas_call(
        mark_kernel,
        out_shape=jax.ShapeDtypeStruct((8, 128), f32),
        in_specs=[pl.BlockSpec(memory_space=pl.ANY)] * len(arrays),
        compiler_params=pltpu.CompilerParams(vmem_limit_bytes=1 << 20),
        name="mark",
    )(*arrays)


def head_kernel(slots, rows_ref, weight_ref, bias_ref, mine_ref, other_ref, rows, part):
    labels, width = weight_ref.shape
    lanes = width // 128 + 1
    me, core = number(), lax.axis_size("doc")
    rows[...] = rows_ref[...].astype(f32)
    weight = weight_ref[...]
    embed = jnp.concatenate([rows[:, k, :] for k in range(lanes - 1)], axis=1)
    logits = lax.dot_general(
        embed.astype(bf16), weight, (((1,), (1,)), ((), ())), preferred_element_type=f32
    ) + bias_ref[...].astype(f32).reshape(1, labels)
    digits = rows[:, lanes - 1, :]
    ids = digits[:, :slots] * (PIECE * PIECE) + digits[:, slots : 2 * slots] * PIECE + digits[:, 2 * slots : 3 * slots]
    own = lax.broadcasted_iota(jnp.int32, logits.shape, 1) + (me * labels + 1)
    listed = ids.astype(jnp.int32)
    hit = own == listed[:, 0:1]
    for k in range(1, slots):
        hit = jnp.logical_or(hit, own == listed[:, k : k + 1])
    d_logit = (jax.nn.sigmoid(logits) - jnp.where(hit, 1.0, 0.0)).astype(bf16)
    part[...] = jnp.dot(d_logit, weight, preferred_element_type=f32)
    half = part.shape[0] // 2
    kind = lax.rem(me // core, 2)
    mine_ref[...] = part[pl.ds(pl.multiple_of(kind * half, half), half), :]
    other_ref[...] = part[pl.ds(pl.multiple_of((1 - kind) * half, half), half), :]


def share(first, acts, d_pre, factors, gains, weight_ref, out_ref, act):
    half, width = act.shape[1], d_pre.shape[1]
    columns = pl.ds(first, half)
    base = 0
    for ref in acts:
        act[pl.ds(base, ref.shape[0]), :] = ref[:, columns]
        base += ref.shape[0]
    left, right = factors
    even = lax.dot_general(left[:, columns], right[...], (((0,), (0,)), ((), ())), preferred_element_type=f32)
    total = even + lax.dot_general(act[...], d_pre[...], (((0,), (0,)), ((), ())), preferred_element_type=f32)
    out_ref[:half, :] = total.astype(bf16)
    weighed = total * weight_ref[columns, :].astype(f32)
    lanes = weighed[:, :128]
    for k in range(1, width // 128):
        lanes = lanes + weighed[:, k * 128 : (k + 1) * 128]
    gain_in = jnp.sum(lanes.T, axis=0, keepdims=True) / gains[:, columns]
    none = jnp.zeros((1, width - half), f32)
    return jnp.concatenate([none, gain_in] if first else [gain_in, none], axis=1)


def terms(values):
    parts = []
    for rest in values:
        for _ in range(3):
            parts.append(rest.astype(bf16).astype(f32))
            rest = rest - parts[-1]
    return jnp.concatenate(parts + [jnp.zeros((16 - len(parts), rest.shape[1]), f32)], axis=0).astype(bf16)


def back_kernel(seq, masks, *refs):
    grad_ref, gains_ref, weight_ref = refs[:3]
    groups = [refs[3 + 3 * g : 6 + 3 * g] for g in range(len(masks))]
    out_ref, own_ref, d_pre, left, right, act, saved, spreads, own, sem = refs[3 + 3 * len(masks) :]
    me, core = number(), lax.axis_size("doc")
    places = [[place(me ^ m, core) for m in group] for group in masks]
    own[...] = grad_ref[pl.ds(place(me, core), 1), :]
    copy = pltpu.make_async_copy(own, own_ref, sem)
    copy.start()
    half = weight_ref.shape[0] // 2
    for (_, _, row_ref), group in zip(groups, places, strict=True):
        for d, at in enumerate(group):
            saved[at] = row_ref[d]
    row, normed, inverse, sums = grad_ref[...], saved[:, 0, :], saved[:, 1, :], saved[:, 2, :]
    d_normed = row * gains_ref[1:2, :]
    spread = (
        inverse
        * (
            d_normed
            - jnp.mean(d_normed, axis=-1, keepdims=True)
            - normed * jnp.mean(d_normed * normed, axis=-1, keepdims=True)
        )
        * (1.0 / seq)
    )
    spreads[...] = spread
    even = 0.5 * spread
    sums_top, even_top = sums.astype(bf16), even.astype(bf16)
    sums_low = (sums - sums_top.astype(f32)).astype(bf16)
    even_low = (even - even_top.astype(f32)).astype(bf16)
    left[...] = jnp.concatenate([sums_top, sums_top, sums_low], axis=0)
    right[...] = jnp.concatenate([even_top, even_low, even_top], axis=0)
    base = 0
    for (_, tilt_ref, _), group in zip(groups, places, strict=True):
        for d, at in enumerate(group):
            d_pre[pl.ds(base, seq), :] = (tilt_ref[d * seq : (d + 1) * seq, :] * spreads[pl.ds(at, 1), :]).astype(bf16)
            base += seq
    acts = [act_ref for act_ref, _, _ in groups]
    gain_in = share(0, acts, d_pre, (left, right), gains_ref[0:1, :], weight_ref, out_ref, act)
    out_ref[half:, :] = terms([jnp.sum(row * normed, axis=0, keepdims=True), gain_in])
    copy.wait()


def more_kernel(*refs):
    (gains_ref, weight_ref, d_pre, left, right), acts, (out_ref, act) = refs[:5], refs[5:-2], refs[-2:]
    half = weight_ref.shape[0] // 2
    gain_in = share(half, acts, d_pre, (left, right), gains_ref[0:1, :], weight_ref, out_ref, act)
    out_ref[half:, :] = terms([jnp.zeros_like(gain_in), gain_in])


def back_calls(seq, masks, total, gains, weight, groups):
    width, docs = weight.shape[0], sum(len(group) for group in masks)
    half = width // 2
    share_shape = jax.ShapeDtypeStruct((half + 16, width), bf16)
    act, vmem = pltpu.VMEM((docs * seq, half), bf16), pl.BlockSpec(memory_space=pltpu.VMEM)
    top, row_grad, *middle = pl.pallas_call(
        functools.partial(back_kernel, seq, masks),
        out_shape=[
            share_shape,
            jax.ShapeDtypeStruct((1, width), f32),
            jax.ShapeDtypeStruct((docs * seq, width), bf16),
            jax.ShapeDtypeStruct((3 * docs, width), bf16),
            jax.ShapeDtypeStruct((3 * docs, width), bf16),
        ],
        out_specs=[vmem, pl.BlockSpec(memory_space=pltpu.HBM), vmem, vmem, vmem],
        scratch_shapes=[
            act,
            pltpu.VMEM((docs, 8, width), f32),
            pltpu.VMEM((docs, width), f32),
            pltpu.VMEM((1, width), f32),
            pltpu.SemaphoreType.DMA,
        ],
        compiler_params=pltpu.CompilerParams(vmem_limit_bytes=32 << 20),
        name="back",
    )(total, gains, weight, *[array for group in groups for array in group])
    low = pl.pallas_call(
        more_kernel,
        out_shape=share_shape,
        scratch_shapes=[act],
        compiler_params=pltpu.CompilerParams(vmem_limit_bytes=24 << 20),
        name="more",
    )(gains, weight, *middle, *[group[0] for group in groups])
    return top, low, row_grad


def final_kernel(first, *refs):
    (mine_ref, other_ref), weight_ref, (total, gains, sems) = refs[:2], refs[-4 - (first > 0)], refs[-3:]
    rows, steps = total.shape[0], sems.shape[0] - 1
    span = rows // steps
    copies = []
    if first:
        gain_in = gain_out = 0.0
        for pair in (refs[:2], refs[2:4]):
            mine, other = pair[0][rows:, :].astype(f32), pair[1][rows:, :].astype(f32)
            gain_out += (mine[0:1] + mine[1:2] + mine[2:3]) + (other[0:1] + other[1:2] + other[2:3])
            gain_in += (mine[3:4] + mine[4:5] + mine[5:6]) + (other[3:4] + other[4:5] + other[5:6])
        gains[...] = jnp.concatenate([gain_in, gain_out], axis=0)
        copies.append(pltpu.make_async_copy(gains, refs[-4], sems.at[steps]))
        copies[-1].start()
    for k in range(steps):
        part = pl.ds(k * span, span)
        total[part, :] = mine_ref[part, :].astype(f32) + other_ref[part, :].astype(f32)
        copies.append(pltpu.make_async_copy(total.at[part, :], weight_ref.at[pl.ds(first + k * span, span), :], sems.at[k]))
        copies[-1].start()
    for copy in copies:
        copy.wait()


def final_call(first, shares, before=None):
    rows, width = shares[0].shape[0] - 16, shares[0].shape[1]
    steps = 4 if rows % 64 == 0 else 1
    vmem, hbm = pl.BlockSpec(memory_space=pltpu.VMEM), pl.BlockSpec(memory_space=pltpu.HBM)
    extra = [] if before is None else [before]
    return pl.pallas_call(
        functools.partial(final_kernel, first),
        out_shape=[jax.ShapeDtypeStruct((2 * rows, width), f32)] + [jax.ShapeDtypeStruct((2, width), f32)] * len(extra),
        in_specs=[vmem] * len(shares) + [hbm] * len(extra),
        out_specs=[hbm] * (1 + len(extra)),
        input_output_aliases={len(shares): 0} if extra else {},
        scratch_shapes=[
            pltpu.VMEM((rows, width), f32),
            pltpu.VMEM((2, width), f32),
            pltpu.SemaphoreType.DMA((steps + 1,)),
        ],
        compiler_params=pltpu.CompilerParams(vmem_limit_bytes=12 << 20),
        name="final",
    )(*shares, *extra)


def swap(value, mask, count):
    return lax.ppermute(value, AXES, [(i, i ^ mask) for i in range(count)])


def combos(bits):
    masks = [0]
    for bit in bits:
        masks += [m | bit for m in masks]
    return masks


def gathered(tokens, norm_gains, enc_weight, head_weight, head_bias, positives):
    n_doc, count = lax.axis_size("doc"), lax.axis_size(AXES)
    seq, width = tokens.shape[1:]
    slots = positives.shape[1]
    core = n_doc
    bits = [1 << b for b in range(count.bit_length() - 1) if 1 << b != core]
    x, y, z, far = bits
    hop = functools.partial(swap, count=count)
    half, h = count // 2, seq // 2
    by_core = [i for i in range(count) if not i & core] + [i for i in range(count) if i & core]

    own = tokens.reshape(seq, width)
    held = {0: [(own, 0, seq)]}

    def exchange(plan, tied=()):
        come = {}
        for to, wanted in plan.items():
            parts = []
            for doc, low, high in wanted:
                at = 0
                for array, first, rows in held[doc]:
                    start, stop = max(low, at), min(high, at + rows)
                    if start < stop:
                        parts.append((array, first + start - at, stop - start))
                    at += rows
            come[to] = hop(parts[0][0] if not tied else join(parts, tied), to)
        new = {}
        for to, wanted in plan.items():
            at = 0
            for doc, low, high in wanted:
                new.setdefault(doc ^ to, []).append((low, come[to], at, high - low))
                at += high - low
        fresh = {}
        for doc, pieces in new.items():
            fresh[doc] = [piece[1:] for piece in sorted(pieces, key=lambda piece: piece[0])]
        held.update(fresh)
        return list(fresh), list(come.values())

    groups, masks = [], []

    def encode_held(docs):
        arrays, layout = [], []
        for doc in docs:
            pieces = []
            for array, first, rows in held[doc]:
                known = [k for k, a in enumerate(arrays) if a is array]
                if not known:
                    known = [len(arrays)]
                    arrays.append(array)
                pieces.append((known[0], first, rows))
            layout.append(pieces)
        groups.append(encode_call(arrays, layout, norm_gains, enc_weight))
        masks.append(docs)
        return groups[-1][2]

    whole = (0, 0, seq)
    docs_0, _ = exchange({far: [whole], z: [whole], x: [whole], y: [whole]})
    *group, copies = first_call(own, norm_gains, enc_weight, positives, count)
    groups.append(group)
    masks.append([0])
    rows = lax.all_to_all(copies, AXES, split_axis=0, concat_axis=0, tiled=True, axis_index_groups=[by_core])

    def spread(full, corners):
        wanted = [(doc, 0, seq) for doc in full]
        return {
            x: wanted + [(y | doc, 0, h) for doc in corners],
            y: wanted + [(x | doc, h, seq) for doc in corners],
        }

    early = mark([held[far][0][0], held[z][0][0]])
    plan = spread([z, far], [0])
    plan[z] = [(far, 0, seq)]
    docs_1, _ = exchange(plan, [groups[0][2], early])
    mine, other = pl.pallas_call(
        functools.partial(head_kernel, slots),
        out_shape=[jax.ShapeDtypeStruct((half, width), f32)] * 2,
        scratch_shapes=[pltpu.VMEM(rows.shape, f32), pltpu.VMEM((count, width), f32)],
        compiler_params=pltpu.CompilerParams(vmem_limit_bytes=10 << 20),
        name="head",
    )(rows, head_weight, head_bias)

    total = add([mine, hop(other, core)])
    plan = spread([z | far], [z, far])
    docs_2, _ = exchange(plan, [total])
    tied = encode_held(docs_0)
    total = add([total, hop(total, z)], [tied])
    tied = encode_held(docs_1[:5])
    total = add([total, hop(total, far)], [tied])
    plan = spread([], [z | far])
    docs_3, _ = exchange(plan, [total])
    rest = docs_1[5:]
    tied = [encode_held(rest)] if rest else []
    total = add([total, hop(total, x)], tied)
    tied = [encode_held(docs_2), encode_held(docs_3)]
    total = add([total, hop(total, y)], tied)

    top, low, row_grad = back_calls(seq, masks, total, norm_gains, enc_weight, groups)
    other_top, other_low = hop(top, core), hop(low, core)
    (weight_grad,) = final_call(0, [top, other_top])
    weight_grad, gain_grads = final_call(width // 2, [low, other_low, top, other_top], weight_grad)
    return row_grad, weight_grad, gain_grads


def normalize(values):
    center = values - jnp.mean(values, axis=-1, keepdims=True)
    inverse = lax.rsqrt(jnp.mean(center * center, axis=-1, keepdims=True) + epsilon)
    return (center * inverse, inverse)


def encode(tok_block, gains, enc_weight):
    width = tok_block.shape[-1]
    tok_flat = tok_block.reshape(-1, width).astype(f32)
    normed_in, _ = normalize(tok_flat)
    act_in = (normed_in * gains[0]).astype(bf16)
    pre_act = jnp.dot(act_in, enc_weight, preferred_element_type=f32)
    hidden = tok_flat + jax.nn.gelu(pre_act)
    pooled = jnp.mean(hidden.reshape(tok_block.shape[0], tok_block.shape[1], width), axis=1)
    normed_out, inv_out = normalize(pooled)
    return (normed_out * gains[1], (normed_in, act_in, pre_act, normed_out, inv_out))


def encode_back(cotangent, saved, gains, enc_weight, seq_len):
    normed_in, act_in, pre_act, normed_out, inv_out = saved
    gain_out_grad = jnp.sum(cotangent * normed_out, axis=0)
    d_normed = cotangent * gains[1]
    d_pooled = inv_out * (
        d_normed
        - jnp.mean(d_normed, axis=-1, keepdims=True)
        - normed_out * jnp.mean(d_normed * normed_out, axis=-1, keepdims=True)
    )
    spread_grad = jnp.broadcast_to(
        (d_pooled / seq_len)[:, None, :], (d_pooled.shape[0], seq_len, d_pooled.shape[1])
    ).reshape(pre_act.shape)
    _, gelu_back = jax.vjp(jax.nn.gelu, pre_act)
    d_pre = gelu_back(spread_grad)[0]
    weight_grad = lax.dot_general(
        act_in.astype(f32), d_pre, (((0,), (0,)), ((), ())), precision=lax.Precision.HIGHEST, preferred_element_type=f32
    )
    d_act = lax.dot_general(
        d_pre, enc_weight.astype(f32), (((1,), (1,)), ((), ())), precision=lax.Precision.HIGHEST, preferred_element_type=f32
    )
    gain_in_grad = jnp.sum(d_act * normed_in, axis=0)
    return (weight_grad, jnp.stack([gain_in_grad, gain_out_grad]))


def head_block(embed_bf, label_lists, weight_block, bias_block, first_label):
    logits = lax.dot_general(embed_bf, weight_block, (((1,), (1,)), ((), ())), preferred_element_type=f32)
    logits = logits + bias_block.astype(f32)[None, :]
    label_ids = first_label + jnp.arange(weight_block.shape[0], dtype=jnp.int32)
    target = jnp.any(label_lists[:, :, None] == label_ids[None, None, :], axis=1).astype(f32)
    d_logit = (jax.nn.sigmoid(logits) - target).astype(bf16)
    return jnp.dot(d_logit, weight_block, preferred_element_type=f32)


def spread_out(tokens, norm_gains, enc_weight, head_weight, head_bias, positives):
    doc_count, seq_len, width = tokens.shape
    embed, saved = encode(tokens, norm_gains, enc_weight)
    col_embed, col_lists = (
        lax.all_gather(embed.astype(bf16), "label", axis=0, tiled=True),
        lax.all_gather(positives, "label", axis=0, tiled=True),
    )
    span = head_weight.shape[0] * lax.axis_size("doc")
    partial_grad = head_block(
        col_embed,
        col_lists,
        lax.all_gather(head_weight, "doc", axis=0, tiled=True),
        lax.all_gather(head_bias, "doc", axis=0, tiled=True),
        lax.axis_index("label") * span,
    )
    summed = lax.psum(partial_grad, "label")
    row_grad = lax.dynamic_slice_in_dim(summed, lax.axis_index("label") * doc_count, doc_count, 0)
    weight_part, gain_part = encode_back(row_grad, saved, norm_gains, enc_weight, seq_len)
    weight_grad, gain_grads = lax.psum((weight_part, gain_part), AXES)
    return (row_grad, weight_grad, gain_grads)


def shards(tokens, *rest):
    count = lax.axis_size(AXES)
    powers = all(size & (size - 1) == 0 for size in (count, lax.axis_size("doc")))
    fits = tokens.size * tokens.dtype.itemsize * (count // 2) <= GATHER_LIMIT
    plan = gathered if fits and powers and count == 32 and tokens.shape[0] == 1 else spread_out
    return plan(tokens, *rest)


def solution(mesh):
    placed = (
        P(AXES, None, None),
        P(),
        P(),
        P(AXES, None),
        P(AXES),
        P(AXES, None),
    )
    return jax.shard_map(
        shards,
        mesh=mesh,
        in_specs=placed,
        out_specs=(P(AXES, None), P(), P()),
        check_vma=False,
    )
```

```python
import functools
import math

import jax
import jax.numpy as jnp
from jax import lax
from jax.experimental import pallas as pl
from jax.experimental.pallas import tpu as pltpu
from jax.sharding import PartitionSpec as P

epsilon = 1e-05
AXES = ("label", "doc")
PIECE_BITS = 8
PIECE = 1 << PIECE_BITS
DIGITS = 3
GATHER_LIMIT = 8 << 20
FIRST_LIMIT = 10 << 20
f32, bf16 = jnp.float32, jnp.bfloat16


def enter(tok, gains):
    values = tok.astype(f32)
    center = values - jnp.mean(values, axis=-1, keepdims=True)
    inverse = lax.rsqrt(jnp.mean(center * center, axis=-1, keepdims=True) + epsilon)
    act = (center * inverse * gains[0:1]).astype(bf16)
    return act, jnp.sum(act.astype(f32), axis=0, keepdims=True)


def bend(tok, pre):
    scale = math.sqrt(2.0 / math.pi)
    square = pre * pre
    half = 0.5 * jnp.tanh(pre * (scale + (scale * 0.044715) * square))
    gelu = pre * (0.5 + half)
    tilt = half + gelu * (0.5 - half) * (2.0 * scale + (6.0 * scale * 0.044715) * square)
    return tilt, jnp.sum(tok.astype(f32) + gelu, axis=0, keepdims=True)


def norm_row(pooled):
    center = pooled - jnp.mean(pooled, axis=-1, keepdims=True)
    inverse = lax.rsqrt(jnp.mean(center * center, axis=-1, keepdims=True) + epsilon)
    return center * inverse, inverse


def place(device, core):
    return (device // (2 * core)) * core + device % core


def number():
    return lax.axis_index("label") * lax.axis_size("doc") + lax.axis_index("doc")


def encode_into(layout, toks, gains, weight, act_ref, tilt_ref, row_ref):
    seq = sum(rows for _, _, rows in layout[0])
    span = seq // 2
    halves = []
    for doc in layout:
        for operand, first, rows in doc:
            halves += [(operand, first + start) for start in range(0, rows, span)]
    acts = []
    for k, (operand, first) in enumerate(halves):
        act, sums = enter(toks[operand][first : first + span, :], gains)
        act_ref[k * span : (k + 1) * span, :] = act
        acts.append(sums)
    totals = []
    for k, (operand, first) in enumerate(halves):
        if k % 2 == 0:
            pre = jnp.dot(act_ref[k * span : (k + 2) * span, :], weight, preferred_element_type=f32)
        tilt, sums = bend(toks[operand][first : first + span, :], pre[k % 2 * span : (k % 2 + 1) * span])
        tilt_ref[k * span : (k + 1) * span, :] = tilt
        totals.append(sums)
    for d in range(len(layout)):
        normed, inverse = norm_row((totals[2 * d] + totals[2 * d + 1]) * (1.0 / seq))
        row_ref[d, 0:1, :] = normed
        row_ref[d, 1:2, :] = jnp.broadcast_to(inverse, normed.shape)
        row_ref[d, 2:3, :] = acts[2 * d] + acts[2 * d + 1]
    return normed


def first_kernel(*refs):
    sources, (act_ref, tilt_ref, row_ref, embed_ref), held, (digits, sems) = refs[:4], refs[4:8], refs[8:12], refs[12:]
    copies = [pltpu.make_async_copy(a, b, sems.at[k]) for k, (a, b) in enumerate(zip(sources, held, strict=True))]
    for copy in copies:
        copy.start()
    for copy in copies:
        copy.wait()
    tok, gains_ref, weight_ref, listed_ref = held
    gains = gains_ref[...]
    seq, width = tok.shape
    slots = listed_ref.shape[1]
    normed = encode_into([[(0, 0, seq)]], [tok], gains, weight_ref[...], act_ref, tilt_ref, row_ref)
    embed = normed * gains[1:2]
    digits[...] = jnp.zeros_like(digits)
    shifted = listed_ref[...] + 1
    for k in range(DIGITS):
        digit = jnp.bitwise_and(jnp.right_shift(shifted, PIECE_BITS * (DIGITS - 1 - k)), PIECE - 1)
        digits[:, k * slots : (k + 1) * slots] = digit.astype(f32)
    lanes = [embed[:, k * 128 : (k + 1) * 128] for k in range(width // 128)] + [digits[...]]
    lanes += [jnp.zeros((1, 128), f32)] * (embed_ref.shape[1] - len(lanes))
    block = jnp.concatenate(lanes, axis=0).astype(bf16)
    embed_ref[...] = jnp.broadcast_to(block[None], embed_ref.shape)


def encode_kernel(layout, *refs):
    toks, (gains_ref, weight_ref, act_ref, tilt_ref, row_ref) = refs[:-5], refs[-5:]
    encode_into(layout, toks, gains_ref[...], weight_ref[...], act_ref, tilt_ref, row_ref)


def encode_shapes(rows, docs, width):
    return [
        jax.ShapeDtypeStruct((rows, width), bf16),
        jax.ShapeDtypeStruct((rows, width), f32),
        jax.ShapeDtypeStruct((docs, 8, width), f32),
    ]


def first_call(own, gains, weight, listed, copies):
    seq, width = own.shape
    sources = [own, gains, weight, listed]
    deep = -(-(width // 128 + 1) // 8) * 8
    return pl.pallas_call(
        first_kernel,
        out_shape=encode_shapes(seq, 1, width) + [jax.ShapeDtypeStruct((copies, deep, 128), bf16)],
        in_specs=[pl.BlockSpec(memory_space=pltpu.HBM)] * 4,
        scratch_shapes=[pltpu.VMEM(a.shape, a.dtype) for a in sources]
        + [pltpu.VMEM((1, 128), f32), pltpu.SemaphoreType.DMA((4,))],
        compiler_params=pltpu.CompilerParams(vmem_limit_bytes=FIRST_LIMIT),
        name="first",
    )(*sources)


def encode_call(arrays, layout, gains, weight):
    rows = sum(piece[2] for doc in layout for piece in doc)
    return pl.pallas_call(
        functools.partial(encode_kernel, layout),
        out_shape=encode_shapes(rows, len(layout), gains.shape[1]),
        compiler_params=pltpu.CompilerParams(vmem_limit_bytes=14 << 20),
        name="encode",
    )(*arrays, gains, weight)


def join_kernel(pieces, *refs):
    out_ref = refs[-1]
    at = 0
    for operand, first, rows in pieces:
        out_ref[at : at + rows, :] = refs[operand][first : first + rows, :]
        at += rows


def join(parts, tied=()):
    arrays, pieces = [], []
    for array, first, rows in parts:
        known = [k for k, a in enumerate(arrays) if a is array]
        if not known:
            known = [len(arrays)]
            arrays.append(array)
        pieces.append((known[0], first, rows))
    vmem, anywhere = pl.BlockSpec(memory_space=pltpu.VMEM), pl.BlockSpec(memory_space=pl.ANY)
    return pl.pallas_call(
        functools.partial(join_kernel, pieces),
        out_shape=jax.ShapeDtypeStruct((sum(p[2] for p in pieces), arrays[0].shape[1]), arrays[0].dtype),
        in_specs=[vmem] * len(arrays) + [anywhere] * len(tied),
        compiler_params=pltpu.CompilerParams(vmem_limit_bytes=4 << 20),
        name="join",
    )(*arrays, *tied)


def add_kernel(count, *refs):
    parts = [ref[...] for ref in refs[:count]]
    while len(parts) > 1:
        parts = [parts[i] + parts[i + 1] for i in range(0, len(parts), 2)]
    refs[-1][...] = parts[0]


def add(parts, tied=()):
    vmem, anywhere = pl.BlockSpec(memory_space=pltpu.VMEM), pl.BlockSpec(memory_space=pl.ANY)
    return pl.pallas_call(
        functools.partial(add_kernel, len(parts)),
        out_shape=jax.ShapeDtypeStruct(parts[0].shape, parts[0].dtype),
        in_specs=[vmem] * len(parts) + [anywhere] * len(tied),
        compiler_params=pltpu.CompilerParams(vmem_limit_bytes=4 << 20),
        name="add",
    )(*parts, *tied)


def mark_kernel(*refs):
    refs[-1][...] = jnp.zeros_like(refs[-1])


def mark(arrays):
    return pl.pallas_call(
        mark_kernel,
        out_shape=jax.ShapeDtypeStruct((8, 128), f32),
        in_specs=[pl.BlockSpec(memory_space=pl.ANY)] * len(arrays),
        compiler_params=pltpu.CompilerParams(vmem_limit_bytes=1 << 20),
        name="mark",
    )(*arrays)


def head_kernel(slots, rows_ref, weight_ref, bias_ref, mine_ref, other_ref, rows, part):
    labels, width = weight_ref.shape
    lanes = width // 128 + 1
    me, core = number(), lax.axis_size("doc")
    rows[...] = rows_ref[...].astype(f32)
    weight = weight_ref[...]
    embed = jnp.concatenate([rows[:, k, :] for k in range(lanes - 1)], axis=1)
    logits = lax.dot_general(
        embed.astype(bf16), weight, (((1,), (1,)), ((), ())), preferred_element_type=f32
    ) + bias_ref[...].astype(f32).reshape(1, labels)
    digits = rows[:, lanes - 1, :]
    ids = digits[:, :slots] * (PIECE * PIECE) + digits[:, slots : 2 * slots] * PIECE + digits[:, 2 * slots : 3 * slots]
    own = lax.broadcasted_iota(jnp.int32, logits.shape, 1) + (me * labels + 1)
    listed = ids.astype(jnp.int32)
    hit = own == listed[:, 0:1]
    for k in range(1, slots):
        hit = jnp.logical_or(hit, own == listed[:, k : k + 1])
    d_logit = (jax.nn.sigmoid(logits) - jnp.where(hit, 1.0, 0.0)).astype(bf16)
    part[...] = jnp.dot(d_logit, weight, preferred_element_type=f32)
    half = part.shape[0] // 2
    kind = lax.rem(me // core, 2)
    mine_ref[...] = part[pl.ds(pl.multiple_of(kind * half, half), half), :]
    other_ref[...] = part[pl.ds(pl.multiple_of((1 - kind) * half, half), half), :]


def share(first, acts, d_pre, factors, gains, weight_ref, out_ref, act, fill=None):
    half, width = act.shape[1], d_pre.shape[1]
    columns = pl.ds(first, half)
    left, right = factors
    total = lax.dot_general(left[:, columns], right[...], (((0,), (0,)), ((), ())), preferred_element_type=f32)
    base = cut = 0
    for k, ref in enumerate(acts):
        if fill is not None:
            fill(k)
        act[pl.ds(base, ref.shape[0]), :] = ref[:, columns]
        base += ref.shape[0]
        if base - cut >= act.shape[0] // 2 or base == act.shape[0]:
            part = pl.ds(cut, base - cut)
            total = total + lax.dot_general(
                act[part, :], d_pre[part, :], (((0,), (0,)), ((), ())), preferred_element_type=f32
            )
            cut = base
    out_ref[:half, :] = total.astype(bf16)
    weighed = total * weight_ref[columns, :].astype(f32)
    lanes = weighed[:, :128]
    for k in range(1, width // 128):
        lanes = lanes + weighed[:, k * 128 : (k + 1) * 128]
    gain_in = jnp.sum(lanes.T, axis=0, keepdims=True) / gains[:, columns]
    none = jnp.zeros((1, width - half), f32)
    return jnp.concatenate([none, gain_in] if first else [gain_in, none], axis=1)


def terms(values):
    parts = []
    for rest in values:
        for _ in range(3):
            parts.append(rest.astype(bf16).astype(f32))
            rest = rest - parts[-1]
    return jnp.concatenate(parts + [jnp.zeros((16 - len(parts), rest.shape[1]), f32)], axis=0).astype(bf16)


def back_kernel(seq, masks, *refs):
    grad_ref, gains_ref, weight_ref = refs[:3]
    groups = [refs[3 + 3 * g : 6 + 3 * g] for g in range(len(masks))]
    out_ref, own_ref, d_pre, left, right, act, saved, spreads, own, sem = refs[3 + 3 * len(masks) :]
    me, core = number(), lax.axis_size("doc")
    places = [[place(me ^ m, core) for m in group] for group in masks]
    own[...] = grad_ref[pl.ds(place(me, core), 1), :]
    copy = pltpu.make_async_copy(own, own_ref, sem)
    copy.start()
    half = weight_ref.shape[0] // 2
    for (_, _, row_ref), group in zip(groups, places, strict=True):
        for d, at in enumerate(group):
            saved[at] = row_ref[d]
    row, normed, inverse, sums = grad_ref[...], saved[:, 0, :], saved[:, 1, :], saved[:, 2, :]
    d_normed = row * gains_ref[1:2, :]
    spread = (
        inverse
        * (
            d_normed
            - jnp.mean(d_normed, axis=-1, keepdims=True)
            - normed * jnp.mean(d_normed * normed, axis=-1, keepdims=True)
        )
        * (1.0 / seq)
    )
    spreads[...] = spread
    even = 0.5 * spread
    sums_top, even_top = sums.astype(bf16), even.astype(bf16)
    sums_low = (sums - sums_top.astype(f32)).astype(bf16)
    even_low = (even - even_top.astype(f32)).astype(bf16)
    left[...] = jnp.concatenate([sums_top, sums_top, sums_low], axis=0)
    right[...] = jnp.concatenate([even_top, even_low, even_top], axis=0)
    starts = [seq * sum(len(group) for group in masks[:g]) for g in range(len(masks))]

    def fill(g):
        tilt_ref = groups[g][1]
        for d, at in enumerate(places[g]):
            rows = pl.ds(d * seq, seq)
            d_pre[pl.ds(starts[g] + d * seq, seq), :] = (tilt_ref[rows, :] * spreads[pl.ds(at, 1), :]).astype(bf16)

    acts = [act_ref for act_ref, _, _ in groups]
    gain_in = share(0, acts, d_pre, (left, right), gains_ref[0:1, :], weight_ref, out_ref, act, fill)
    out_ref[half:, :] = terms([jnp.sum(row * normed, axis=0, keepdims=True), gain_in])
    copy.wait()


def more_kernel(*refs):
    (gains_ref, weight_ref, d_pre, left, right), acts, (out_ref, act) = refs[:5], refs[5:-2], refs[-2:]
    half = weight_ref.shape[0] // 2
    gain_in = share(half, acts, d_pre, (left, right), gains_ref[0:1, :], weight_ref, out_ref, act)
    out_ref[half:, :] = terms([jnp.zeros_like(gain_in), gain_in])


def back_calls(seq, masks, total, gains, weight, groups):
    width, docs = weight.shape[0], sum(len(group) for group in masks)
    half = width // 2
    share_shape = jax.ShapeDtypeStruct((half + 16, width), bf16)
    act, vmem = pltpu.VMEM((docs * seq, half), bf16), pl.BlockSpec(memory_space=pltpu.VMEM)
    top, row_grad, *middle = pl.pallas_call(
        functools.partial(back_kernel, seq, masks),
        out_shape=[
            share_shape,
            jax.ShapeDtypeStruct((1, width), f32),
            jax.ShapeDtypeStruct((docs * seq, width), bf16),
            jax.ShapeDtypeStruct((3 * docs, width), bf16),
            jax.ShapeDtypeStruct((3 * docs, width), bf16),
        ],
        out_specs=[vmem, pl.BlockSpec(memory_space=pltpu.HBM), vmem, vmem, vmem],
        scratch_shapes=[
            act,
            pltpu.VMEM((docs, 8, width), f32),
            pltpu.VMEM((docs, width), f32),
            pltpu.VMEM((1, width), f32),
            pltpu.SemaphoreType.DMA,
        ],
        compiler_params=pltpu.CompilerParams(vmem_limit_bytes=32 << 20),
        name="back",
    )(total, gains, weight, *[array for group in groups for array in group])
    low = pl.pallas_call(
        more_kernel,
        out_shape=share_shape,
        scratch_shapes=[act],
        compiler_params=pltpu.CompilerParams(vmem_limit_bytes=24 << 20),
        name="more",
    )(gains, weight, *middle, *[group[0] for group in groups])
    return top, low, row_grad


def final_kernel(first, *refs):
    (mine_ref, other_ref), weight_ref, (total, gains, sems) = refs[:2], refs[-4 - (first > 0)], refs[-3:]
    rows, steps = total.shape[0], sems.shape[0] - 1
    span = rows // steps
    copies = []
    if first:
        gain_in = gain_out = 0.0
        for pair in (refs[:2], refs[2:4]):
            mine, other = pair[0][rows:, :].astype(f32), pair[1][rows:, :].astype(f32)
            gain_out += (mine[0:1] + mine[1:2] + mine[2:3]) + (other[0:1] + other[1:2] + other[2:3])
            gain_in += (mine[3:4] + mine[4:5] + mine[5:6]) + (other[3:4] + other[4:5] + other[5:6])
        gains[...] = jnp.concatenate([gain_in, gain_out], axis=0)
        copies.append(pltpu.make_async_copy(gains, refs[-4], sems.at[steps]))
        copies[-1].start()
    for k in range(steps):
        part = pl.ds(k * span, span)
        total[part, :] = mine_ref[part, :].astype(f32) + other_ref[part, :].astype(f32)
        copies.append(pltpu.make_async_copy(total.at[part, :], weight_ref.at[pl.ds(first + k * span, span), :], sems.at[k]))
        copies[-1].start()
    for copy in copies:
        copy.wait()


def final_call(first, shares, before=None):
    rows, width = shares[0].shape[0] - 16, shares[0].shape[1]
    steps = 4 if rows % 64 == 0 else 1
    vmem, hbm = pl.BlockSpec(memory_space=pltpu.VMEM), pl.BlockSpec(memory_space=pltpu.HBM)
    extra = [] if before is None else [before]
    return pl.pallas_call(
        functools.partial(final_kernel, first),
        out_shape=[jax.ShapeDtypeStruct((2 * rows, width), f32)] + [jax.ShapeDtypeStruct((2, width), f32)] * len(extra),
        in_specs=[vmem] * len(shares) + [hbm] * len(extra),
        out_specs=[hbm] * (1 + len(extra)),
        input_output_aliases={len(shares): 0} if extra else {},
        scratch_shapes=[
            pltpu.VMEM((rows, width), f32),
            pltpu.VMEM((2, width), f32),
            pltpu.SemaphoreType.DMA((steps + 1,)),
        ],
        compiler_params=pltpu.CompilerParams(vmem_limit_bytes=12 << 20),
        name="final",
    )(*shares, *extra)


def swap(value, mask, count):
    return lax.ppermute(value, AXES, [(i, i ^ mask) for i in range(count)])


def combos(bits):
    masks = [0]
    for bit in bits:
        masks += [m | bit for m in masks]
    return masks


def gathered(tokens, norm_gains, enc_weight, head_weight, head_bias, positives):
    n_doc, count = lax.axis_size("doc"), lax.axis_size(AXES)
    seq, width = tokens.shape[1:]
    slots = positives.shape[1]
    core = n_doc
    bits = [1 << b for b in range(count.bit_length() - 1) if 1 << b != core]
    x, y, z, far = bits
    hop = functools.partial(swap, count=count)
    half, h = count // 2, seq // 2
    by_core = [i for i in range(count) if not i & core] + [i for i in range(count) if i & core]

    own = tokens.reshape(seq, width)
    held = {0: [(own, 0, seq)]}

    def exchange(plan, tied=()):
        come = {}
        for to, wanted in plan.items():
            parts = []
            for doc, low, high in wanted:
                at = 0
                for array, first, rows in held[doc]:
                    start, stop = max(low, at), min(high, at + rows)
                    if start < stop:
                        parts.append((array, first + start - at, stop - start))
                    at += rows
            come[to] = hop(parts[0][0] if not tied else join(parts, tied), to)
        new = {}
        for to, wanted in plan.items():
            at = 0
            for doc, low, high in wanted:
                new.setdefault(doc ^ to, []).append((low, come[to], at, high - low))
                at += high - low
        fresh = {}
        for doc, pieces in new.items():
            fresh[doc] = [piece[1:] for piece in sorted(pieces, key=lambda piece: piece[0])]
        held.update(fresh)
        return list(fresh), list(come.values())

    groups, masks = [], []

    def encode_held(docs):
        arrays, layout = [], []
        for doc in docs:
            pieces = []
            for array, first, rows in held[doc]:
                known = [k for k, a in enumerate(arrays) if a is array]
                if not known:
                    known = [len(arrays)]
                    arrays.append(array)
                pieces.append((known[0], first, rows))
            layout.append(pieces)
        groups.append(encode_call(arrays, layout, norm_gains, enc_weight))
        masks.append(docs)
        return groups[-1][2]

    whole = (0, 0, seq)
    docs_0, _ = exchange({far: [whole], z: [whole], x: [whole], y: [whole]})
    *group, copies = first_call(own, norm_gains, enc_weight, positives, count)
    groups.append(group)
    masks.append([0])
    rows = lax.all_to_all(copies, AXES, split_axis=0, concat_axis=0, tiled=True, axis_index_groups=[by_core])

    def spread(full, corners):
        wanted = [(doc, 0, seq) for doc in full]
        return {
            x: wanted + [(y | doc, 0, h) for doc in corners],
            y: wanted + [(x | doc, h, seq) for doc in corners],
        }

    early = mark([held[far][0][0], held[z][0][0]])
    plan = spread([z, far], [0])
    plan[z] = [(far, 0, seq)]
    docs_1, _ = exchange(plan, [groups[0][2], early])
    mine, other = pl.pallas_call(
        functools.partial(head_kernel, slots),
        out_shape=[jax.ShapeDtypeStruct((half, width), f32)] * 2,
        scratch_shapes=[pltpu.VMEM(rows.shape, f32), pltpu.VMEM((count, width), f32)],
        compiler_params=pltpu.CompilerParams(vmem_limit_bytes=10 << 20),
        name="head",
    )(rows, head_weight, head_bias)

    total = add([mine, hop(other, core)])
    plan = spread([z | far], [z, far])
    docs_2, _ = exchange(plan, [total])
    tied = encode_held(docs_0)
    total = add([total, hop(total, z)], [tied])
    tied = encode_held(docs_1[:5])
    total = add([total, hop(total, far)], [tied])
    plan = spread([], [z | far])
    docs_3, _ = exchange(plan, [total])
    rest = docs_1[5:]
    tied = [encode_held(rest)] if rest else []
    total = add([total, hop(total, x)], tied)
    tied = [encode_held(docs_2), encode_held(docs_3)]
    total = add([total, hop(total, y)], tied)

    top, low, row_grad = back_calls(seq, masks, total, norm_gains, enc_weight, groups)
    other_top, other_low = hop(top, core), hop(low, core)
    (weight_grad,) = final_call(0, [top, other_top])
    weight_grad, gain_grads = final_call(width // 2, [low, other_low, top, other_top], weight_grad)
    return row_grad, weight_grad, gain_grads


def normalize(values):
    center = values - jnp.mean(values, axis=-1, keepdims=True)
    inverse = lax.rsqrt(jnp.mean(center * center, axis=-1, keepdims=True) + epsilon)
    return (center * inverse, inverse)


def encode(tok_block, gains, enc_weight):
    width = tok_block.shape[-1]
    tok_flat = tok_block.reshape(-1, width).astype(f32)
    normed_in, _ = normalize(tok_flat)
    act_in = (normed_in * gains[0]).astype(bf16)
    pre_act = jnp.dot(act_in, enc_weight, preferred_element_type=f32)
    hidden = tok_flat + jax.nn.gelu(pre_act)
    pooled = jnp.mean(hidden.reshape(tok_block.shape[0], tok_block.shape[1], width), axis=1)
    normed_out, inv_out = normalize(pooled)
    return (normed_out * gains[1], (normed_in, act_in, pre_act, normed_out, inv_out))


def encode_back(cotangent, saved, gains, enc_weight, seq_len):
    normed_in, act_in, pre_act, normed_out, inv_out = saved
    gain_out_grad = jnp.sum(cotangent * normed_out, axis=0)
    d_normed = cotangent * gains[1]
    d_pooled = inv_out * (
        d_normed
        - jnp.mean(d_normed, axis=-1, keepdims=True)
        - normed_out * jnp.mean(d_normed * normed_out, axis=-1, keepdims=True)
    )
    spread_grad = jnp.broadcast_to(
        (d_pooled / seq_len)[:, None, :], (d_pooled.shape[0], seq_len, d_pooled.shape[1])
    ).reshape(pre_act.shape)
    _, gelu_back = jax.vjp(jax.nn.gelu, pre_act)
    d_pre = gelu_back(spread_grad)[0]
    weight_grad = lax.dot_general(
        act_in.astype(f32), d_pre, (((0,), (0,)), ((), ())), precision=lax.Precision.HIGHEST, preferred_element_type=f32
    )
    d_act = lax.dot_general(
        d_pre, enc_weight.astype(f32), (((1,), (1,)), ((), ())), precision=lax.Precision.HIGHEST, preferred_element_type=f32
    )
    gain_in_grad = jnp.sum(d_act * normed_in, axis=0)
    return (weight_grad, jnp.stack([gain_in_grad, gain_out_grad]))


def head_block(embed_bf, label_lists, weight_block, bias_block, first_label):
    logits = lax.dot_general(embed_bf, weight_block, (((1,), (1,)), ((), ())), preferred_element_type=f32)
    logits = logits + bias_block.astype(f32)[None, :]
    label_ids = first_label + jnp.arange(weight_block.shape[0], dtype=jnp.int32)
    target = jnp.any(label_lists[:, :, None] == label_ids[None, None, :], axis=1).astype(f32)
    d_logit = (jax.nn.sigmoid(logits) - target).astype(bf16)
    return jnp.dot(d_logit, weight_block, preferred_element_type=f32)


def spread_out(tokens, norm_gains, enc_weight, head_weight, head_bias, positives):
    doc_count, seq_len, width = tokens.shape
    embed, saved = encode(tokens, norm_gains, enc_weight)
    col_embed, col_lists = (
        lax.all_gather(embed.astype(bf16), "label", axis=0, tiled=True),
        lax.all_gather(positives, "label", axis=0, tiled=True),
    )
    span = head_weight.shape[0] * lax.axis_size("doc")
    partial_grad = head_block(
        col_embed,
        col_lists,
        lax.all_gather(head_weight, "doc", axis=0, tiled=True),
        lax.all_gather(head_bias, "doc", axis=0, tiled=True),
        lax.axis_index("label") * span,
    )
    summed = lax.psum(partial_grad, "label")
    row_grad = lax.dynamic_slice_in_dim(summed, lax.axis_index("label") * doc_count, doc_count, 0)
    weight_part, gain_part = encode_back(row_grad, saved, norm_gains, enc_weight, seq_len)
    weight_grad, gain_grads = lax.psum((weight_part, gain_part), AXES)
    return (row_grad, weight_grad, gain_grads)


def shards(tokens, *rest):
    count = lax.axis_size(AXES)
    powers = all(size & (size - 1) == 0 for size in (count, lax.axis_size("doc")))
    fits = tokens.size * tokens.dtype.itemsize * (count // 2) <= GATHER_LIMIT
    plan = gathered if fits and powers and count == 32 and tokens.shape[0] == 1 else spread_out
    return plan(tokens, *rest)


def solution(mesh):
    placed = (
        P(AXES, None, None),
        P(),
        P(),
        P(AXES, None),
        P(AXES),
        P(AXES, None),
    )
    return jax.shard_map(
        shards,
        mesh=mesh,
        in_specs=placed,
        out_specs=(P(AXES, None), P(), P()),
        check_vma=False,
    )
```

```python
import functools
import math

import jax
import jax.numpy as jnp
from jax import lax
from jax.experimental import pallas as pl
from jax.experimental.pallas import tpu as pltpu
from jax.sharding import PartitionSpec as P

epsilon = 1e-05
AXES = ("label", "doc")
PIECE_BITS = 8
PIECE = 1 << PIECE_BITS
DIGITS = 3
GATHER_LIMIT = 8 << 20
FIRST_LIMIT = 10 << 20
f32, bf16 = jnp.float32, jnp.bfloat16


def enter(tok, gains):
    values = tok.astype(f32)
    center = values - jnp.mean(values, axis=-1, keepdims=True)
    inverse = lax.rsqrt(jnp.mean(center * center, axis=-1, keepdims=True) + epsilon)
    act = (center * inverse * gains[0:1]).astype(bf16)
    return act, jnp.sum(act.astype(f32), axis=0, keepdims=True)


def bend(tok, pre):
    scale = math.sqrt(2.0 / math.pi)
    square = pre * pre
    half = 0.5 * jnp.tanh(pre * (scale + (scale * 0.044715) * square))
    gelu = pre * (0.5 + half)
    tilt = half + gelu * (0.5 - half) * (2.0 * scale + (6.0 * scale * 0.044715) * square)
    return tilt, jnp.sum(tok.astype(f32) + gelu, axis=0, keepdims=True)


def norm_row(pooled):
    center = pooled - jnp.mean(pooled, axis=-1, keepdims=True)
    inverse = lax.rsqrt(jnp.mean(center * center, axis=-1, keepdims=True) + epsilon)
    return center * inverse, inverse


def place(device, core):
    return (device // (2 * core)) * core + device % core


def number():
    return lax.axis_index("label") * lax.axis_size("doc") + lax.axis_index("doc")


def encode_into(layout, toks, gains, weight, act_ref, tilt_ref, row_ref):
    seq = sum(rows for _, _, rows in layout[0])
    span = seq // 2
    halves = []
    for doc in layout:
        for operand, first, rows in doc:
            halves += [(operand, first + start) for start in range(0, rows, span)]
    acts = []
    for k, (operand, first) in enumerate(halves):
        act, sums = enter(toks[operand][first : first + span, :], gains)
        act_ref[k * span : (k + 1) * span, :] = act
        acts.append(sums)
    totals = []
    for k, (operand, first) in enumerate(halves):
        if k % 2 == 0:
            pre = jnp.dot(act_ref[k * span : (k + 2) * span, :], weight, preferred_element_type=f32)
        tilt, sums = bend(toks[operand][first : first + span, :], pre[k % 2 * span : (k % 2 + 1) * span])
        tilt_ref[k * span : (k + 1) * span, :] = tilt
        totals.append(sums)
    for d in range(len(layout)):
        normed, inverse = norm_row((totals[2 * d] + totals[2 * d + 1]) * (1.0 / seq))
        row_ref[d, 0:1, :] = normed
        row_ref[d, 1:2, :] = jnp.broadcast_to(inverse, normed.shape)
        row_ref[d, 2:3, :] = acts[2 * d] + acts[2 * d + 1]
    return normed


def first_kernel(*refs):
    sources, (act_ref, tilt_ref, row_ref, embed_ref), held, (digits, sems) = refs[:4], refs[4:8], refs[8:12], refs[12:]
    copies = [pltpu.make_async_copy(a, b, sems.at[k]) for k, (a, b) in enumerate(zip(sources, held, strict=True))]
    for copy in copies:
        copy.start()
    for copy in copies:
        copy.wait()
    tok, gains_ref, weight_ref, listed_ref = held
    gains = gains_ref[...]
    seq, width = tok.shape
    slots = listed_ref.shape[1]
    normed = encode_into([[(0, 0, seq)]], [tok], gains, weight_ref[...], act_ref, tilt_ref, row_ref)
    embed = normed * gains[1:2]
    digits[...] = jnp.zeros_like(digits)
    shifted = listed_ref[...] + 1
    for k in range(DIGITS):
        digit = jnp.bitwise_and(jnp.right_shift(shifted, PIECE_BITS * (DIGITS - 1 - k)), PIECE - 1)
        digits[:, k * slots : (k + 1) * slots] = digit.astype(f32)
    lanes = [embed[:, k * 128 : (k + 1) * 128] for k in range(width // 128)] + [digits[...]]
    lanes += [jnp.zeros((1, 128), f32)] * (embed_ref.shape[1] - len(lanes))
    block = jnp.concatenate(lanes, axis=0).astype(bf16)
    embed_ref[...] = jnp.broadcast_to(block[None], embed_ref.shape)


def encode_kernel(layout, *refs):
    toks, (gains_ref, weight_ref, act_ref, tilt_ref, row_ref) = refs[:-5], refs[-5:]
    encode_into(layout, toks, gains_ref[...], weight_ref[...], act_ref, tilt_ref, row_ref)


def encode_shapes(rows, docs, width):
    return [
        jax.ShapeDtypeStruct((rows, width), bf16),
        jax.ShapeDtypeStruct((rows, width), f32),
        jax.ShapeDtypeStruct((docs, 8, width), f32),
    ]


def first_call(own, gains, weight, listed, copies):
    seq, width = own.shape
    sources = [own, gains, weight, listed]
    deep = -(-(width // 128 + 1) // 8) * 8
    return pl.pallas_call(
        first_kernel,
        out_shape=encode_shapes(seq, 1, width) + [jax.ShapeDtypeStruct((copies, deep, 128), bf16)],
        in_specs=[pl.BlockSpec(memory_space=pltpu.HBM)] * 4,
        scratch_shapes=[pltpu.VMEM(a.shape, a.dtype) for a in sources]
        + [pltpu.VMEM((1, 128), f32), pltpu.SemaphoreType.DMA((4,))],
        compiler_params=pltpu.CompilerParams(vmem_limit_bytes=FIRST_LIMIT),
        name="first",
    )(*sources)


def encode_call(arrays, layout, gains, weight):
    rows = sum(piece[2] for doc in layout for piece in doc)
    return pl.pallas_call(
        functools.partial(encode_kernel, layout),
        out_shape=encode_shapes(rows, len(layout), gains.shape[1]),
        compiler_params=pltpu.CompilerParams(vmem_limit_bytes=14 << 20),
        name="encode",
    )(*arrays, gains, weight)


def join_kernel(pieces, *refs):
    out_ref = refs[-1]
    at = 0
    for operand, first, rows in pieces:
        out_ref[at : at + rows, :] = refs[operand][first : first + rows, :]
        at += rows


def join(parts, tied=()):
    arrays, pieces = [], []
    for array, first, rows in parts:
        known = [k for k, a in enumerate(arrays) if a is array]
        if not known:
            known = [len(arrays)]
            arrays.append(array)
        pieces.append((known[0], first, rows))
    vmem, anywhere = pl.BlockSpec(memory_space=pltpu.VMEM), pl.BlockSpec(memory_space=pl.ANY)
    return pl.pallas_call(
        functools.partial(join_kernel, pieces),
        out_shape=jax.ShapeDtypeStruct((sum(p[2] for p in pieces), arrays[0].shape[1]), arrays[0].dtype),
        in_specs=[vmem] * len(arrays) + [anywhere] * len(tied),
        compiler_params=pltpu.CompilerParams(vmem_limit_bytes=4 << 20),
        name="join",
    )(*arrays, *tied)


def add_kernel(count, *refs):
    parts = [ref[...] for ref in refs[:count]]
    while len(parts) > 1:
        parts = [parts[i] + parts[i + 1] for i in range(0, len(parts), 2)]
    refs[-1][...] = parts[0]


def add(parts, tied=()):
    vmem, anywhere = pl.BlockSpec(memory_space=pltpu.VMEM), pl.BlockSpec(memory_space=pl.ANY)
    return pl.pallas_call(
        functools.partial(add_kernel, len(parts)),
        out_shape=jax.ShapeDtypeStruct(parts[0].shape, parts[0].dtype),
        in_specs=[vmem] * len(parts) + [anywhere] * len(tied),
        compiler_params=pltpu.CompilerParams(vmem_limit_bytes=4 << 20),
        name="add",
    )(*parts, *tied)


def mark_kernel(*refs):
    refs[-1][...] = jnp.zeros_like(refs[-1])


def mark(arrays):
    return pl.pallas_call(
        mark_kernel,
        out_shape=jax.ShapeDtypeStruct((8, 128), f32),
        in_specs=[pl.BlockSpec(memory_space=pl.ANY)] * len(arrays),
        compiler_params=pltpu.CompilerParams(vmem_limit_bytes=1 << 20),
        name="mark",
    )(*arrays)


def head_kernel(slots, rows_ref, weight_ref, bias_ref, mine_ref, other_ref, rows, part):
    labels, width = weight_ref.shape
    lanes = width // 128 + 1
    me, core = number(), lax.axis_size("doc")
    rows[...] = rows_ref[...].astype(f32)
    weight = weight_ref[...]
    embed = jnp.concatenate([rows[:, k, :] for k in range(lanes - 1)], axis=1)
    logits = lax.dot_general(
        embed.astype(bf16), weight, (((1,), (1,)), ((), ())), preferred_element_type=f32
    ) + bias_ref[...].astype(f32).reshape(1, labels)
    digits = rows[:, lanes - 1, :]
    ids = digits[:, :slots] * (PIECE * PIECE) + digits[:, slots : 2 * slots] * PIECE + digits[:, 2 * slots : 3 * slots]
    own = lax.broadcasted_iota(jnp.int32, logits.shape, 1) + (me * labels + 1)
    listed = ids.astype(jnp.int32)
    hit = own == listed[:, 0:1]
    for k in range(1, slots):
        hit = jnp.logical_or(hit, own == listed[:, k : k + 1])
    d_logit = (jax.nn.sigmoid(logits) - jnp.where(hit, 1.0, 0.0)).astype(bf16)
    part[...] = jnp.dot(d_logit, weight, preferred_element_type=f32)
    half = part.shape[0] // 2
    kind = lax.rem(me // core, 2)
    mine_ref[...] = part[pl.ds(pl.multiple_of(kind * half, half), half), :]
    other_ref[...] = part[pl.ds(pl.multiple_of((1 - kind) * half, half), half), :]


def share(first, acts, d_pre, factors, gains, weight_ref, out_ref, act):
    half, width = act.shape[1], d_pre.shape[1]
    columns = pl.ds(first, half)
    base = 0
    for ref in acts:
        act[pl.ds(base, ref.shape[0]), :] = ref[:, columns]
        base += ref.shape[0]
    left, right = factors
    even = lax.dot_general(left[:, columns], right[...], (((0,), (0,)), ((), ())), preferred_element_type=f32)
    total = even + lax.dot_general(act[...], d_pre[...], (((0,), (0,)), ((), ())), preferred_element_type=f32)
    out_ref[:half, :] = total.astype(bf16)
    weighed = total * weight_ref[columns, :].astype(f32)
    lanes = weighed[:, :128]
    for k in range(1, width // 128):
        lanes = lanes + weighed[:, k * 128 : (k + 1) * 128]
    gain_in = jnp.sum(lanes.T, axis=0, keepdims=True) / gains[:, columns]
    none = jnp.zeros((1, width - half), f32)
    return jnp.concatenate([none, gain_in] if first else [gain_in, none], axis=1)


def terms(values):
    parts = []
    for rest in values:
        for _ in range(3):
            parts.append(rest.astype(bf16).astype(f32))
            rest = rest - parts[-1]
    return jnp.concatenate(parts + [jnp.zeros((16 - len(parts), rest.shape[1]), f32)], axis=0).astype(bf16)


def back_kernel(seq, masks, *refs):
    grad_ref, gains_ref, weight_ref = refs[:3]
    groups = [refs[3 + 3 * g : 6 + 3 * g] for g in range(len(masks))]
    out_ref, own_ref, d_pre, left, right, act, saved, spreads, own, sem = refs[3 + 3 * len(masks) :]
    me, core = number(), lax.axis_size("doc")
    places = [[place(me ^ m, core) for m in group] for group in masks]
    own[...] = grad_ref[pl.ds(place(me, core), 1), :]
    copy = pltpu.make_async_copy(own, own_ref, sem)
    copy.start()
    half = weight_ref.shape[0] // 2
    for (_, _, row_ref), group in zip(groups, places, strict=True):
        for d, at in enumerate(group):
            saved[at] = row_ref[d]
    row, normed, inverse, sums = grad_ref[...], saved[:, 0, :], saved[:, 1, :], saved[:, 2, :]
    d_normed = row * gains_ref[1:2, :]
    spread = (
        inverse
        * (
            d_normed
            - jnp.mean(d_normed, axis=-1, keepdims=True)
            - normed * jnp.mean(d_normed * normed, axis=-1, keepdims=True)
        )
        * (1.0 / seq)
    )
    spreads[...] = spread
    even = 0.5 * spread
    sums_top, even_top = sums.astype(bf16), even.astype(bf16)
    sums_low = (sums - sums_top.astype(f32)).astype(bf16)
    even_low = (even - even_top.astype(f32)).astype(bf16)
    left[...] = jnp.concatenate([sums_top, sums_top, sums_low], axis=0)
    right[...] = jnp.concatenate([even_top, even_low, even_top], axis=0)
    base = 0
    for (_, tilt_ref, _), group in zip(groups, places, strict=True):
        for d, at in enumerate(group):
            d_pre[pl.ds(base, seq), :] = (tilt_ref[d * seq : (d + 1) * seq, :] * spreads[pl.ds(at, 1), :]).astype(bf16)
            base += seq
    acts = [act_ref for act_ref, _, _ in groups]
    gain_in = share(0, acts, d_pre, (left, right), gains_ref[0:1, :], weight_ref, out_ref, act)
    out_ref[half:, :] = terms([jnp.sum(row * normed, axis=0, keepdims=True), gain_in])
    copy.wait()


def more_kernel(*refs):
    (gains_ref, weight_ref, d_pre, left, right), acts, (out_ref, act) = refs[:5], refs[5:-2], refs[-2:]
    half = weight_ref.shape[0] // 2
    gain_in = share(half, acts, d_pre, (left, right), gains_ref[0:1, :], weight_ref, out_ref, act)
    out_ref[half:, :] = terms([jnp.zeros_like(gain_in), gain_in])


def back_calls(seq, masks, total, gains, weight, groups):
    width, docs = weight.shape[0], sum(len(group) for group in masks)
    half = width // 2
    share_shape = jax.ShapeDtypeStruct((half + 16, width), bf16)
    act, vmem = pltpu.VMEM((docs * seq, half), bf16), pl.BlockSpec(memory_space=pltpu.VMEM)
    top, row_grad, *middle = pl.pallas_call(
        functools.partial(back_kernel, seq, masks),
        out_shape=[
            share_shape,
            jax.ShapeDtypeStruct((1, width), f32),
            jax.ShapeDtypeStruct((docs * seq, width), bf16),
            jax.ShapeDtypeStruct((3 * docs, width), bf16),
            jax.ShapeDtypeStruct((3 * docs, width), bf16),
        ],
        out_specs=[vmem, pl.BlockSpec(memory_space=pltpu.HBM), vmem, vmem, vmem],
        scratch_shapes=[
            act,
            pltpu.VMEM((docs, 8, width), f32),
            pltpu.VMEM((docs, width), f32),
            pltpu.VMEM((1, width), f32),
            pltpu.SemaphoreType.DMA,
        ],
        compiler_params=pltpu.CompilerParams(vmem_limit_bytes=32 << 20),
        name="back",
    )(total, gains, weight, *[array for group in groups for array in group])
    low = pl.pallas_call(
        more_kernel,
        out_shape=share_shape,
        scratch_shapes=[act],
        compiler_params=pltpu.CompilerParams(vmem_limit_bytes=24 << 20),
        name="more",
    )(gains, weight, *middle, *[group[0] for group in groups])
    return top, low, row_grad


def final_kernel(first, *refs):
    (mine_ref, other_ref), weight_ref, (total, gains, sems) = refs[:2], refs[-4 - (first > 0)], refs[-3:]
    rows, steps = total.shape[0], sems.shape[0] - 1
    span = rows // steps
    copies = []
    if first:
        gain_in = gain_out = 0.0
        for pair in (refs[:2], refs[2:4]):
            mine, other = pair[0][rows:, :].astype(f32), pair[1][rows:, :].astype(f32)
            gain_out += (mine[0:1] + mine[1:2] + mine[2:3]) + (other[0:1] + other[1:2] + other[2:3])
            gain_in += (mine[3:4] + mine[4:5] + mine[5:6]) + (other[3:4] + other[4:5] + other[5:6])
        gains[...] = jnp.concatenate([gain_in, gain_out], axis=0)
        copies.append(pltpu.make_async_copy(gains, refs[-4], sems.at[steps]))
        copies[-1].start()
    for k in range(steps):
        part = pl.ds(k * span, span)
        total[part, :] = mine_ref[part, :].astype(f32) + other_ref[part, :].astype(f32)
        copies.append(pltpu.make_async_copy(total.at[part, :], weight_ref.at[pl.ds(first + k * span, span), :], sems.at[k]))
        copies[-1].start()
    for copy in copies:
        copy.wait()


def final_call(first, shares, before=None):
    rows, width = shares[0].shape[0] - 16, shares[0].shape[1]
    steps = 8 if rows % 128 == 0 else 1
    vmem, hbm = pl.BlockSpec(memory_space=pltpu.VMEM), pl.BlockSpec(memory_space=pltpu.HBM)
    extra = [] if before is None else [before]
    return pl.pallas_call(
        functools.partial(final_kernel, first),
        out_shape=[jax.ShapeDtypeStruct((2 * rows, width), f32)] + [jax.ShapeDtypeStruct((2, width), f32)] * len(extra),
        in_specs=[vmem] * len(shares) + [hbm] * len(extra),
        out_specs=[hbm] * (1 + len(extra)),
        input_output_aliases={len(shares): 0} if extra else {},
        scratch_shapes=[
            pltpu.VMEM((rows, width), f32),
            pltpu.VMEM((2, width), f32),
            pltpu.SemaphoreType.DMA((steps + 1,)),
        ],
        compiler_params=pltpu.CompilerParams(vmem_limit_bytes=12 << 20),
        name="final",
    )(*shares, *extra)


def swap(value, mask, count):
    return lax.ppermute(value, AXES, [(i, i ^ mask) for i in range(count)])


def combos(bits):
    masks = [0]
    for bit in bits:
        masks += [m | bit for m in masks]
    return masks


def gathered(tokens, norm_gains, enc_weight, head_weight, head_bias, positives):
    n_doc, count = lax.axis_size("doc"), lax.axis_size(AXES)
    seq, width = tokens.shape[1:]
    slots = positives.shape[1]
    core = n_doc
    bits = [1 << b for b in range(count.bit_length() - 1) if 1 << b != core]
    x, y, z, far = bits
    hop = functools.partial(swap, count=count)
    half, h = count // 2, seq // 2
    by_core = [i for i in range(count) if not i & core] + [i for i in range(count) if i & core]

    own = tokens.reshape(seq, width)
    held = {0: [(own, 0, seq)]}

    def exchange(plan, tied=()):
        come = {}
        for to, wanted in plan.items():
            parts = []
            for doc, low, high in wanted:
                at = 0
                for array, first, rows in held[doc]:
                    start, stop = max(low, at), min(high, at + rows)
                    if start < stop:
                        parts.append((array, first + start - at, stop - start))
                    at += rows
            come[to] = hop(parts[0][0] if not tied else join(parts, tied), to)
        new = {}
        for to, wanted in plan.items():
            at = 0
            for doc, low, high in wanted:
                new.setdefault(doc ^ to, []).append((low, come[to], at, high - low))
                at += high - low
        fresh = {}
        for doc, pieces in new.items():
            fresh[doc] = [piece[1:] for piece in sorted(pieces, key=lambda piece: piece[0])]
        held.update(fresh)
        return list(fresh), list(come.values())

    groups, masks = [], []

    def encode_held(docs):
        arrays, layout = [], []
        for doc in docs:
            pieces = []
            for array, first, rows in held[doc]:
                known = [k for k, a in enumerate(arrays) if a is array]
                if not known:
                    known = [len(arrays)]
                    arrays.append(array)
                pieces.append((known[0], first, rows))
            layout.append(pieces)
        groups.append(encode_call(arrays, layout, norm_gains, enc_weight))
        masks.append(docs)
        return groups[-1][2]

    whole = (0, 0, seq)
    docs_0, _ = exchange({far: [whole], z: [whole], x: [whole], y: [whole]})
    *group, copies = first_call(own, norm_gains, enc_weight, positives, count)
    groups.append(group)
    masks.append([0])
    rows = lax.all_to_all(copies, AXES, split_axis=0, concat_axis=0, tiled=True, axis_index_groups=[by_core])

    def spread(full, corners):
        wanted = [(doc, 0, seq) for doc in full]
        return {
            x: wanted + [(y | doc, 0, h) for doc in corners],
            y: wanted + [(x | doc, h, seq) for doc in corners],
        }

    early = mark([held[far][0][0], held[z][0][0]])
    plan = spread([z, far], [0])
    plan[z] = [(far, 0, seq)]
    docs_1, _ = exchange(plan, [groups[0][2], early])
    mine, other = pl.pallas_call(
        functools.partial(head_kernel, slots),
        out_shape=[jax.ShapeDtypeStruct((half, width), f32)] * 2,
        scratch_shapes=[pltpu.VMEM(rows.shape, f32), pltpu.VMEM((count, width), f32)],
        compiler_params=pltpu.CompilerParams(vmem_limit_bytes=10 << 20),
        name="head",
    )(rows, head_weight, head_bias)

    total = add([mine, hop(other, core)])
    plan = spread([z | far], [z, far])
    docs_2, _ = exchange(plan, [total])
    tied = encode_held(docs_0)
    total = add([total, hop(total, z)], [tied])
    tied = encode_held(docs_1[:5])
    total = add([total, hop(total, far)], [tied])
    plan = spread([], [z | far])
    docs_3, _ = exchange(plan, [total])
    rest = docs_1[5:]
    tied = [encode_held(rest)] if rest else []
    total = add([total, hop(total, x)], tied)
    tied = [encode_held(docs_2), encode_held(docs_3)]
    total = add([total, hop(total, y)], tied)

    top, low, row_grad = back_calls(seq, masks, total, norm_gains, enc_weight, groups)
    other_top, other_low = hop(top, core), hop(low, core)
    (weight_grad,) = final_call(0, [top, other_top])
    weight_grad, gain_grads = final_call(width // 2, [low, other_low, top, other_top], weight_grad)
    return row_grad, weight_grad, gain_grads


def normalize(values):
    center = values - jnp.mean(values, axis=-1, keepdims=True)
    inverse = lax.rsqrt(jnp.mean(center * center, axis=-1, keepdims=True) + epsilon)
    return (center * inverse, inverse)


def encode(tok_block, gains, enc_weight):
    width = tok_block.shape[-1]
    tok_flat = tok_block.reshape(-1, width).astype(f32)
    normed_in, _ = normalize(tok_flat)
    act_in = (normed_in * gains[0]).astype(bf16)
    pre_act = jnp.dot(act_in, enc_weight, preferred_element_type=f32)
    hidden = tok_flat + jax.nn.gelu(pre_act)
    pooled = jnp.mean(hidden.reshape(tok_block.shape[0], tok_block.shape[1], width), axis=1)
    normed_out, inv_out = normalize(pooled)
    return (normed_out * gains[1], (normed_in, act_in, pre_act, normed_out, inv_out))


def encode_back(cotangent, saved, gains, enc_weight, seq_len):
    normed_in, act_in, pre_act, normed_out, inv_out = saved
    gain_out_grad = jnp.sum(cotangent * normed_out, axis=0)
    d_normed = cotangent * gains[1]
    d_pooled = inv_out * (
        d_normed
        - jnp.mean(d_normed, axis=-1, keepdims=True)
        - normed_out * jnp.mean(d_normed * normed_out, axis=-1, keepdims=True)
    )
    spread_grad = jnp.broadcast_to(
        (d_pooled / seq_len)[:, None, :], (d_pooled.shape[0], seq_len, d_pooled.shape[1])
    ).reshape(pre_act.shape)
    _, gelu_back = jax.vjp(jax.nn.gelu, pre_act)
    d_pre = gelu_back(spread_grad)[0]
    weight_grad = lax.dot_general(
        act_in.astype(f32), d_pre, (((0,), (0,)), ((), ())), precision=lax.Precision.HIGHEST, preferred_element_type=f32
    )
    d_act = lax.dot_general(
        d_pre, enc_weight.astype(f32), (((1,), (1,)), ((), ())), precision=lax.Precision.HIGHEST, preferred_element_type=f32
    )
    gain_in_grad = jnp.sum(d_act * normed_in, axis=0)
    return (weight_grad, jnp.stack([gain_in_grad, gain_out_grad]))


def head_block(embed_bf, label_lists, weight_block, bias_block, first_label):
    logits = lax.dot_general(embed_bf, weight_block, (((1,), (1,)), ((), ())), preferred_element_type=f32)
    logits = logits + bias_block.astype(f32)[None, :]
    label_ids = first_label + jnp.arange(weight_block.shape[0], dtype=jnp.int32)
    target = jnp.any(label_lists[:, :, None] == label_ids[None, None, :], axis=1).astype(f32)
    d_logit = (jax.nn.sigmoid(logits) - target).astype(bf16)
    return jnp.dot(d_logit, weight_block, preferred_element_type=f32)


def spread_out(tokens, norm_gains, enc_weight, head_weight, head_bias, positives):
    doc_count, seq_len, width = tokens.shape
    embed, saved = encode(tokens, norm_gains, enc_weight)
    col_embed, col_lists = (
        lax.all_gather(embed.astype(bf16), "label", axis=0, tiled=True),
        lax.all_gather(positives, "label", axis=0, tiled=True),
    )
    span = head_weight.shape[0] * lax.axis_size("doc")
    partial_grad = head_block(
        col_embed,
        col_lists,
        lax.all_gather(head_weight, "doc", axis=0, tiled=True),
        lax.all_gather(head_bias, "doc", axis=0, tiled=True),
        lax.axis_index("label") * span,
    )
    summed = lax.psum(partial_grad, "label")
    row_grad = lax.dynamic_slice_in_dim(summed, lax.axis_index("label") * doc_count, doc_count, 0)
    weight_part, gain_part = encode_back(row_grad, saved, norm_gains, enc_weight, seq_len)
    weight_grad, gain_grads = lax.psum((weight_part, gain_part), AXES)
    return (row_grad, weight_grad, gain_grads)


def shards(tokens, *rest):
    count = lax.axis_size(AXES)
    powers = all(size & (size - 1) == 0 for size in (count, lax.axis_size("doc")))
    fits = tokens.size * tokens.dtype.itemsize * (count // 2) <= GATHER_LIMIT
    plan = gathered if fits and powers and count == 32 and tokens.shape[0] == 1 else spread_out
    return plan(tokens, *rest)


def solution(mesh):
    placed = (
        P(AXES, None, None),
        P(),
        P(),
        P(AXES, None),
        P(AXES),
        P(AXES, None),
    )
    return jax.shard_map(
        shards,
        mesh=mesh,
        in_specs=placed,
        out_specs=(P(AXES, None), P(), P()),
        check_vma=False,
    )
```
